256 devices in a mesh: mem: 8 (over x, core), grid: 32 (over y, z).
Axes of the slice: x: 4, y: 4, z: 8, core: 2. Of those that a mesh axis runs over, the one named last changes fastest.
Arguments:
- prior: float32 [320, 2, 16, 2, 1280], P('grid', None, 'mem'), may hold values from -120 to 120
- posterior: float32 [320, 2, 16, 2, 1280], P('grid', None, 'mem'), may hold values from -120 to 120
- cycle_rows: int32 [320], replicated, may hold values from 0 to 319, each once
- relaxation: float32 [2], replicated, may hold values from 0.3 to 0.95
Outputs:
- inflated: float32 [320, 2, 16, 2, 1280], P('grid', None, 'mem')
The draws below stay inside these ranges and needn't reach their ends.
All inputs are finite; a program needn't handle non-finite values.
Results may differ from the reference program's by a relative error of at most 0.0023.
Values sent between devices are 32-bit elements; how exact they have to be, the bound alone decides.
A program may use at most 192 MiB of HBM per device.

```python
import math
import jax
import jax.numpy as jnp
from jax import lax

NLAT = 640
LEV = 2
NLON = 1280
NPAIR = 320
MEMBERS = 16
N_GRID = 32


def smoothed(noise):
    return 0.5 * (noise + jnp.roll(noise, 1, axis=-1) + jnp.roll(noise, 2, axis=-1) + jnp.roll(noise, 3, axis=-1))


def member_scale(key, spread):
    jitter = jax.random.uniform(key, (MEMBERS,), jnp.float32)
    positions = (jnp.arange(MEMBERS).astype(jnp.float32) + jitter) / MEMBERS
    return jnp.exp(jnp.log(spread) * positions)


def assemble(common, rough_part, smooth_noise, smooth_weight, amplitude, scales, level_gain):
    perturbed = rough_part + smooth_weight * smoothed(smooth_noise)
    factor = amplitude * scales[None, None, :, None, None] * level_gain[None, None, None, :, None]
    return common + factor * perturbed


def draw_prior(key, part):
    key = jax.random.fold_in(key, 11)
    subkeys = jax.random.split(key, 5)
    full_shape = (NPAIR, 2, MEMBERS, LEV, NLON)
    common_shape = (NPAIR, 2, 1, LEV, NLON)
    level_gain = jnp.exp(jax.random.uniform(subkeys[4], (LEV,), jnp.float32, -0.4, 0.4))
    rough_part = jax.random.truncated_normal(subkeys[0], -4.0, 4.0, full_shape, jnp.float32)
    smooth_noise = jax.random.truncated_normal(subkeys[1], -4.0, 4.0, full_shape, jnp.float32)
    common = jax.random.truncated_normal(subkeys[2], -4.0, 4.0, common_shape, jnp.float32)
    scales = member_scale(subkeys[3], 3.0)
    return assemble(common, rough_part, smooth_noise, 2.0, 1.0, scales, level_gain)


def draw_posterior(key, part):
    key = jax.random.fold_in(key, 12)
    subkeys = jax.random.split(key, 5)
    full_shape = (NPAIR, 2, MEMBERS, LEV, NLON)
    common_shape = (NPAIR, 2, 1, LEV, NLON)
    level_gain = jnp.exp(jax.random.uniform(subkeys[4], (LEV,), jnp.float32, -0.4, 0.4))
    rough_part = jax.random.truncated_normal(subkeys[0], -4.0, 4.0, full_shape, jnp.float32)
    smooth_noise = jax.random.truncated_normal(subkeys[1], -4.0, 4.0, full_shape, jnp.float32)
    common = jax.random.truncated_normal(subkeys[2], -4.0, 4.0, common_shape, jnp.float32)
    scales = member_scale(subkeys[3], 3.0)
    return assemble(common, rough_part, smooth_noise, 1.0, 0.6, scales, level_gain)


def setup_inputs(seed: int = 0) -> dict:
    key_of = jax.random.split(jax.random.key(seed), 5)
    prior = draw_prior(jax.random.fold_in(key_of[4], 71), 0)
    posterior = draw_posterior(jax.random.fold_in(key_of[4], 71), 0)
    cycle_rows = jax.random.permutation(key_of[2], NPAIR).astype(jnp.int32)
    relaxation = jnp.clip(jax.random.uniform(key_of[3], (LEV,), jnp.float32, 0.3, 0.95), 0.3, 0.95)
    return dict(prior=prior, posterior=posterior, cycle_rows=cycle_rows, relaxation=relaxation)


precise = lax.Precision.HIGHEST
epsilon = 1e-06

def cycle_terms(cycle_rows, orders):
    colatitude = math.pi * (cycle_rows.astype(jnp.float32) + 0.5) / orders
    sine_values = jnp.sin(colatitude)
    return (jnp.cos(colatitude), sine_values, math.pi / orders * sine_values)

def fourier_angles(grid_count, half_slots, longitudes):
    orders = longitudes // 2
    owners = jnp.arange(grid_count, dtype=jnp.int32)[:, None]
    slot_ids = jnp.arange(2 * half_slots, dtype=jnp.int32)[None, :]
    base_ids = owners * half_slots + slot_ids
    order_ids = jnp.where(slot_ids < half_slots, base_ids, orders - 1 - (base_ids - half_slots))
    points = jnp.arange(longitudes, dtype=jnp.int32)
    phases = points[:, None, None] * order_ids[None, :, :] % longitudes
    angles = 2.0 * math.pi / longitudes * phases.astype(jnp.float32)
    return (order_ids, angles)

def forward_table(angles, longitudes):
    return jnp.stack([jnp.cos(angles), -jnp.sin(angles)], axis=-1).reshape(longitudes, -1)

def inverse_table(order_ids, angles, longitudes):
    weight = jnp.where(order_ids == 0, 2.0, 2.0) * 0.0 + jnp.where(order_ids == 0, 1.0, 2.0)
    weight = weight.astype(angles.dtype)[None, :, :] / longitudes
    stacked = jnp.stack([weight * jnp.cos(angles), -weight * jnp.sin(angles)], axis=-1)
    return jnp.transpose(stacked, (1, 2, 3, 0)).reshape(-1, longitudes)

def legendre_table(pair_ids, cosines, sine_values, orders):
    row_count = orders // 2 + 1
    pair_count = pair_ids.shape[0]
    cycle_count = cosines.shape[0]
    positions = jnp.arange(1, orders + 1).astype(cosines.dtype)
    cumulative_log = jnp.concatenate([jnp.zeros((1,), cosines.dtype), jnp.cumsum(jnp.log((2.0 * positions - 1.0) / (2.0 * positions)))])
    all_orders = jnp.arange(orders + 1, dtype=jnp.int32)
    log_sine = jnp.log(sine_values)
    first_order = pair_ids
    second_order = orders - 1 - pair_ids
    first_length = orders - pair_ids

    def start_log(order_ids):
        matches = all_orders[None, :] == order_ids[:, None]
        partial_log = lax.optimization_barrier(jnp.sum(jnp.where(matches, cumulative_log[None, :], 0.0), axis=1))
        order_real = order_ids.astype(cosines.dtype)
        leading_log = 0.5 * (jnp.log((2.0 * order_real + 1.0) / 2.0) + partial_log)
        return leading_log[:, None] + order_real[:, None] * log_sine[None, :]
    start_first = start_log(first_order)
    start_second = start_log(second_order)
    rescale_log = 18.0 * math.log(10.0)

    def advance(recurrence_state, row_index):
        previous, earlier, scale_log = recurrence_state
        in_first = row_index < first_length
        order_now = jnp.where(in_first, first_order, second_order)
        degree_now = jnp.where(in_first, pair_ids + row_index, row_index - 1)
        restart = ((row_index == 0) | (row_index == first_length))[:, None]
        degree_real = degree_now.astype(cosines.dtype)[:, None]
        order_real = order_now.astype(cosines.dtype)[:, None]
        difference = jnp.maximum(degree_real * degree_real - order_real * order_real, 1.0)
        leading = jnp.sqrt((4.0 * degree_real * degree_real - 1.0) / difference)
        lower = degree_real - 1.0
        trailing = jnp.sqrt(jnp.maximum(lower * lower - order_real * order_real, 0.0) / jnp.maximum(4.0 * lower * lower - 1.0, 1.0))
        current = leading * (cosines[None, :] * previous - trailing * earlier)
        current = jnp.where(restart, 1.0, current)
        earlier = jnp.where(restart, 0.0, previous)
        scale_log = jnp.where(restart, jnp.where(in_first[:, None], start_first, start_second), scale_log)
        too_large = jnp.abs(current) > 1e+18
        current = jnp.where(too_large, current * 1e-18, current)
        earlier = jnp.where(too_large, earlier * 1e-18, earlier)
        scale_log = jnp.where(too_large, scale_log + rescale_log, scale_log)
        entry = jnp.where(row_index <= orders, current * jnp.exp(scale_log), 0.0)
        return ((current, earlier, scale_log), entry)

    def advance_two(recurrence_state, step_index):
        recurrence_state, upper_row = advance(recurrence_state, 2 * step_index)
        recurrence_state, lower_row = advance(recurrence_state, 2 * step_index + 1)
        return (recurrence_state, jnp.stack([upper_row, lower_row], axis=0))
    empty_state = jnp.zeros((pair_count, cycle_count), cosines.dtype)
    final_state, legendre = lax.scan(advance_two, (empty_state, empty_state, empty_state), jnp.arange(row_count, dtype=jnp.int32), unroll=4)
    return legendre

def first_rows(pair_ids, row_count, orders):
    row_ids = 2 * jnp.arange(row_count, dtype=jnp.int32)[None, :] + jnp.arange(2, dtype=jnp.int32)[:, None]
    return row_ids[None, :, :] < (orders - pair_ids)[:, None, None]

def analyse(fourier, legendre, pair_ids, weights, orders):
    half = fourier.shape[0] // 2
    northern = fourier[:, :, :, 0]
    southern = fourier[:, :, :, 1]
    factor = weights[None, None, :, None]
    even_part = (northern + southern) * factor
    odd_part = (northern - southern) * factor
    odd_pairs = (pair_ids % 2 == 1)[:, None, None, None]
    upper_rows = jnp.stack([even_part[:half], jnp.where(odd_pairs, odd_part[half:], even_part[half:])], axis=1)
    lower_rows = jnp.stack([odd_part[:half], jnp.where(odd_pairs, even_part[half:], odd_part[half:])], axis=1)
    stacked = jnp.stack([upper_rows, lower_rows], axis=1)
    result = jnp.einsum('ieqn,qewrnc->qeiwrc', legendre, stacked, precision=precise)
    in_first = first_rows(pair_ids, legendre.shape[0], orders)[:, :, :, None, None]
    return jnp.where(in_first, result[:, :, :, 0], result[:, :, :, 1])

def synthesise(spectral, legendre, pair_ids, orders):
    in_first = first_rows(pair_ids, legendre.shape[0], orders)[:, :, :, None, None]
    placed = jnp.stack([jnp.where(in_first, spectral, 0.0), jnp.where(in_first, 0.0, spectral)], axis=2)
    result = jnp.einsum('ieqn,qewirc->qewrnc', legendre, placed, precision=precise)
    odd_pairs = (pair_ids % 2 == 1)[:, None, None, None]
    even_part = jnp.concatenate([result[:, 0, 0], jnp.where(odd_pairs, result[:, 1, 1], result[:, 0, 1])], axis=0)
    odd_part = jnp.concatenate([result[:, 1, 0], jnp.where(odd_pairs, result[:, 0, 1], result[:, 1, 1])], axis=0)
    return jnp.stack([even_part + odd_part, even_part - odd_part], axis=3)

def degree_power(spectral, pair_ids, orders, levels):
    pair_count, parity, row_count, parts, columns = spectral.shape
    row_span = 2 * row_count
    squares = lax.optimization_barrier(jnp.sum((spectral * spectral).reshape(pair_count, 2, row_count, 2, columns // levels, levels), axis=(3, 4)))
    flattened = jnp.transpose(squares, (0, 3, 2, 1)).reshape(pair_count, levels, row_span)
    row_ids = jnp.arange(row_span, dtype=jnp.int32)
    in_first = (row_ids[None, :] < (orders - pair_ids)[:, None])[:, None, :]
    first_weight = jnp.where(pair_ids == 0, 1.0, 2.0).astype(flattened.dtype)[:, None, None]
    first_part = jnp.where(in_first, flattened, 0.0) * first_weight
    second_part = jnp.where(in_first, 0.0, flattened) * 2.0
    padded = jnp.concatenate([jnp.zeros((pair_count, levels, orders), flattened.dtype), first_part], axis=2)

    def shift(segment, offset):
        return lax.dynamic_slice_in_dim(segment, offset, orders, 1)
    shifted = jax.vmap(shift)(padded, (orders - pair_ids).astype(jnp.int32))
    return lax.optimization_barrier(jnp.sum(shifted, axis=0)) + lax.optimization_barrier(jnp.sum(second_part[:, :, 1:orders + 1], axis=0))

def scale_rows(spectral, inflation_ratio, pair_ids, orders):
    pair_count, parity, row_count, parts, columns = spectral.shape
    levels = inflation_ratio.shape[0]
    row_span = 2 * row_count
    ratio_tail = jnp.concatenate([inflation_ratio, jnp.zeros((levels, row_span), inflation_ratio.dtype)], axis=1)

    def pick(offset):
        return lax.dynamic_slice_in_dim(ratio_tail, offset, row_span, 1)
    first_part = jax.vmap(pick)(pair_ids.astype(jnp.int32))
    edge = jnp.zeros((levels, 1), inflation_ratio.dtype)
    second_part = jnp.concatenate([edge, inflation_ratio, edge], axis=1)
    row_ids = jnp.arange(row_span, dtype=jnp.int32)
    in_first = (row_ids[None, :] < (orders - pair_ids)[:, None])[:, None, :]
    per_row = jnp.where(in_first, first_part, second_part[None, :, :])
    per_row = jnp.transpose(per_row.reshape(pair_count, levels, row_count, 2), (0, 3, 2, 1))
    shaped = spectral.reshape(pair_count, 2, row_count, 2, columns // levels, levels)
    return (shaped * per_row[:, :, :, None, None, :]).reshape(spectral.shape)

def inflation(power_prior, power_post, relaxation, total_members, orders):
    degrees = jnp.arange(orders).astype(power_prior.dtype)[None, :]
    samples = total_members * (2.0 * degrees + 1.0)
    spread_ratio = (power_prior / samples + epsilon) / (power_post / samples + epsilon)
    return (1.0 - relaxation)[:, None] + relaxation[:, None] * jnp.sqrt(spread_ratio)

def reference(prior, posterior, cycle_rows, relaxation):
    half_slots = NPAIR // N_GRID
    columns = MEMBERS * LEV
    contract_dims = (((0,), (1,)), ((), ()))
    mean_prior = lax.optimization_barrier(jnp.sum(prior, axis=2)) / MEMBERS
    mean_post = lax.optimization_barrier(jnp.sum(posterior, axis=2)) / MEMBERS
    order_ids, angles = fourier_angles(N_GRID, half_slots, NLON)
    forward = forward_table(angles, NLON)
    inverse = inverse_table(order_ids, angles, NLON)
    fourier_prior = lax.dot_general(forward, (prior - mean_prior[:, :, None]).reshape(-1, NLON), contract_dims, precision=precise)
    fourier_post = lax.dot_general(forward, (posterior - mean_post[:, :, None]).reshape(-1, NLON), contract_dims, precision=precise)
    blocks_prior = fourier_prior.reshape(N_GRID, 2 * half_slots, 2, NPAIR, 2, columns)
    blocks_post = fourier_post.reshape(N_GRID, 2 * half_slots, 2, NPAIR, 2, columns)
    cosines, sine_values, weights = cycle_terms(cycle_rows, NLAT)
    places = jnp.arange(N_GRID, dtype=jnp.int32)

    def analyse_block(inputs):
        block_prior, block_post, grid_place = inputs
        pair_ids = grid_place * half_slots + jnp.arange(half_slots, dtype=jnp.int32)
        legendre = legendre_table(pair_ids, cosines, sine_values, NLAT)
        spectral_prior = analyse(block_prior, legendre, pair_ids, weights, NLAT)
        spectral_post = analyse(block_post, legendre, pair_ids, weights, NLAT)
        return (spectral_post, degree_power(spectral_prior, pair_ids, NLAT, LEV), degree_power(spectral_post, pair_ids, NLAT, LEV))
    spectral_post, power_prior, power_post = lax.map(analyse_block, (blocks_prior, blocks_post, places))
    inflation_ratio = inflation(lax.optimization_barrier(jnp.sum(power_prior, axis=0)), lax.optimization_barrier(jnp.sum(power_post, axis=0)), relaxation, MEMBERS, NLAT)

    def synth_block(inputs):
        spectral, grid_place = inputs
        pair_ids = grid_place * half_slots + jnp.arange(half_slots, dtype=jnp.int32)
        legendre = legendre_table(pair_ids, cosines, sine_values, NLAT)
        scaled = scale_rows(spectral, inflation_ratio, pair_ids, NLAT)
        return synthesise(scaled, legendre, pair_ids, NLAT)
    returned = lax.map(synth_block, (spectral_post, places))
    grid_values = lax.dot_general(returned.reshape(2 * NLAT, -1), inverse, (((0,), (0,)), ((), ())), precision=precise)
    return grid_values.reshape(NPAIR, 2, MEMBERS, LEV, NLON) + mean_post[:, :, None]
```

```python
import functools
import math

import jax
import jax.numpy as jnp
import ml_dtypes
import numpy as np
from jax import lax
from jax.experimental import pallas as pl
from jax.experimental.pallas import tpu as pltpu
from jax.sharding import PartitionSpec as P

MESH = pl.DeviceIdType.MESH
NLAT = 640
LEV = 2
NLON = 1280
NPAIR = 320
MEMBERS = 16
NG = 32
NM = 8
NY = 4
NZ = 8
HALF = 10
EPS = 1e-06
ROWS = 672
TROWS = 384
BIG = 60 * 1024 * 1024

f32 = jnp.float32
bf16 = jnp.bfloat16


def split_table(table):
    hi = table.astype(np.float32).astype(ml_dtypes.bfloat16)
    lo = (table - hi.astype(np.float64)).astype(np.float32).astype(ml_dtypes.bfloat16)
    return hi, lo


@functools.lru_cache(maxsize=None)
def trig_tables():
    owner = np.arange(NG)[:, None, None]
    pair = np.arange(HALF)[None, :, None]
    segment = np.arange(2)[None, None, :]
    first = owner * HALF + pair
    order = np.where(segment == 0, first, NLAT - 1 - first).reshape(-1)
    phase = (np.arange(NLON)[:, None] * order[None, :]) % NLON
    angle = 2.0 * np.pi / NLON * phase
    table = np.stack([np.cos(angle), -np.sin(angle)], axis=-1).reshape(NLON, NLON)
    weight = np.repeat(np.where(order == 0, 1.0, 2.0) / NLON, 2)
    return split_table(table) + split_table((table * weight[None, :]).T)


@functools.lru_cache(maxsize=None)
def leading_logs():
    i = np.arange(1, NLAT + 1, dtype=np.float64)
    total = np.concatenate([[0.0], np.cumsum(np.log((2 * i - 1) / (2 * i)))])[:NLAT]
    m = np.arange(NLAT, dtype=np.float64)
    return (0.5 * (np.log((2 * m + 1) / 2) + total)).astype(np.float32)


def means_kernel(prior_ref, post_ref, mean_ref, sums, arrived, piece, s1, r1, s2, r2):
    me = lax.axis_index("mem")
    barrier = pltpu.get_barrier_semaphore()
    for k in range(1, NM):
        pl.semaphore_signal(
            barrier, inc=1, device_id={"mem": lax.rem(me + k, NM)}, device_id_type=MESH
        )
    for ens, ref in ((0, prior_ref), (1, post_ref)):
        for j in range(HALF):
            for h in range(2):
                sums[ens * 20 + j * 2 + h] = ref[j, h, 0] + ref[j, h, 1]
    pl.semaphore_wait(barrier, NM - 1)
    copies = []
    for k in range(1, NM):
        peer = lax.rem(me + k, NM)
        copy = pltpu.make_async_remote_copy(
            src_ref=sums.at[pl.ds(peer * 5, 5)],
            dst_ref=arrived.at[NM - 1 - k],
            send_sem=s1.at[k - 1],
            recv_sem=r1.at[k - 1],
            device_id={"mem": peer},
            device_id_type=MESH,
        )
        copy.start()
        copies.append(copy)
    total = sums[pl.ds(me * 5, 5)]
    for k, copy in enumerate(copies):
        copy.wait_recv()
        total = total + arrived[NM - 2 - k]
    piece[...] = total * (1.0 / MEMBERS)
    mean_ref[pl.ds(me * 5, 5)] = piece[...]
    back = []
    for k in range(1, NM):
        peer = lax.rem(me + k, NM)
        copy = pltpu.make_async_remote_copy(
            src_ref=piece,
            dst_ref=mean_ref.at[pl.ds(me * 5, 5)],
            send_sem=s2.at[k - 1],
            recv_sem=r2.at[k - 1],
            device_id={"mem": peer},
            device_id_type=MESH,
        )
        copy.start()
        back.append(copy)
    for copy in copies:
        copy.wait_send()
    for copy in back:
        copy.wait()


def member_means(prior, posterior):
    return pl.pallas_call(
        means_kernel,
        out_shape=jax.ShapeDtypeStruct((40, LEV, NLON), f32),
        in_specs=[pl.BlockSpec(memory_space=pltpu.VMEM)] * 2,
        out_specs=pl.BlockSpec(memory_space=pltpu.VMEM),
        scratch_shapes=[
            pltpu.VMEM((40, LEV, NLON), f32),
            pltpu.VMEM((NM - 1, 5, LEV, NLON), f32),
            pltpu.VMEM((5, LEV, NLON), f32),
            pltpu.SemaphoreType.DMA((NM - 1,)),
            pltpu.SemaphoreType.DMA((NM - 1,)),
            pltpu.SemaphoreType.DMA((NM - 1,)),
            pltpu.SemaphoreType.DMA((NM - 1,)),
        ],
        compiler_params=pltpu.CompilerParams(
            collective_id=0, has_side_effects=True, vmem_limit_bytes=BIG
        ),
        name="member_means",
    )(prior, posterior)


def legendre_kernel(start_ref, cosine_ref, place_ref, table_ref, rows):
    place = place_ref[0]
    zero = jnp.zeros((16, TROWS), f32)
    for i in range(641, ROWS):
        for t in range(3):
            rows[t, i * 16 : i * 16 + 16, :] = zero[:, 0:128]
    sub = lax.broadcasted_iota(jnp.int32, (16, 128), 0)
    step = lax.rem(lax.broadcasted_iota(jnp.int32, (16, 128), 1), 8)
    cosine = jnp.broadcast_to(cosine_ref[...], (16, TROWS))
    pair = place * HALF + sub
    valid = sub < HALF

    def chain(segment, first_block, order):
        def block(b, state):
            current, earlier, scale_log = state
            degree = (b * 8 + step).astype(f32)
            m = order.astype(f32)
            inside = valid & (b * 8 + step > order)
            square = degree * degree
            difference = jnp.where(inside, square - m * m, 1.0)
            low = degree - 1.0
            low_square = low * low
            lead = (4.0 * square - 1.0) / difference
            trail = jnp.maximum(low_square - m * m, 0.0) / jnp.maximum(4.0 * low_square - 1.0, 1.0)
            a = jnp.where(inside, jnp.sqrt(jnp.maximum(lead, 0.0)), 0.0)
            c = jnp.where(inside, a * jnp.sqrt(trail), 0.0)
            d = jnp.where(valid & (b * 8 + step == order), 1.0, 0.0)
            scale = jnp.exp(scale_log)
            for k in range(8):
                ak = jnp.broadcast_to(a[:, k : k + 1], (16, TROWS))
                ck = jnp.broadcast_to(c[:, k : k + 1], (16, TROWS))
                dk = jnp.broadcast_to(d[:, k : k + 1], (16, TROWS))
                following = (ak * cosine) * current + (dk - ck * earlier)
                earlier = current
                current = following
                entry = current * scale
                degree_now = b * 8 + k
                if segment == 0:
                    offset = pl.multiple_of((NLAT - 1 - degree_now) * 16, 16)
                else:
                    offset = pl.multiple_of((degree_now + 1) * 16, 16)
                    second = degree_now >= NLAT - 1 - pair
                for t in range(3):
                    tile = entry[:, t * 128 : t * 128 + 128]
                    if segment == 1:
                        tile = jnp.where(second, tile, rows[t, pl.ds(offset, 16), :])
                    rows[t, pl.ds(offset, 16), :] = tile
            large = jnp.abs(current) > 1e10
            current = jnp.where(large, current * 1e-20, current)
            earlier = jnp.where(large, earlier * 1e-20, earlier)
            scale_log = jnp.where(large, scale_log + 20.0 * math.log(10.0), scale_log)
            return current, earlier, scale_log

        lax.fori_loop(first_block, NLAT // 8, block, (zero, zero, start_ref[segment]))

    chain(0, lax.div(place * HALF, 8), pair)
    chain(1, lax.div(NLAT - HALF - place * HALF, 8), NLAT - 1 - pair)

    right = lax.broadcasted_iota(jnp.int32, (16, 128), 1) < 64
    blank = jnp.zeros((TROWS - ROWS // 2, 640), bf16)
    for p in range(HALF):
        for q in range(2):

            def convert(t, carry):
                out = pl.ds(pl.multiple_of(t * 16, 16), 16)
                for tile in range(3):
                    values = rows[tile, pl.ds(t * 512 + q * 16 + p, 16, stride=32), :]
                    high = values.astype(bf16)
                    low = values - high.astype(f32)
                    if tile < 2:
                        at = tile * 128
                        table_ref[p * 2 + q, out, at : at + 128] = high
                        table_ref[p * 2 + q, out, at + 256 : at + 384] = low.astype(bf16)
                    else:
                        table_ref[p * 2 + q, out, 512:640] = jnp.where(right, values, low).astype(bf16)
                return carry

            lax.fori_loop(0, ROWS // 32, convert, 0, unroll=3)
            table_ref[p * 2 + q, ROWS // 2 : TROWS, :] = blank


def legendre_table(start, cosine, place):
    return pl.pallas_call(
        legendre_kernel,
        out_shape=jax.ShapeDtypeStruct((2 * HALF, TROWS, 640), bf16),
        in_specs=[
            pl.BlockSpec(memory_space=pltpu.VMEM),
            pl.BlockSpec(memory_space=pltpu.VMEM),
            pl.BlockSpec(memory_space=pltpu.SMEM),
        ],
        out_specs=pl.BlockSpec(memory_space=pltpu.VMEM),
        scratch_shapes=[pltpu.VMEM((3, ROWS * 16, 128), f32)],
        compiler_params=pltpu.CompilerParams(vmem_limit_bytes=BIG),
        name="legendre_table",
    )(start, cosine, place)


def split_rows(values):
    high = values.astype(bf16)
    low = (values - high.astype(f32)).astype(bf16)
    return high, low


def forward_kernel(
    prior_ref, post_ref, mean_ref, high_ref, low_ref, out_a, out_b, left, split
):
    @pl.when(pl.program_id(0) == 0)
    def _():
        left[...] = jnp.zeros_like(left)
        for ens, ref in ((0, prior_ref), (1, post_ref)):
            for j in range(HALF):
                north_mean = mean_ref[ens * 20 + j * 2]
                south_mean = mean_ref[ens * 20 + j * 2 + 1]
                for b in range(2):
                    north = ref[j, 0, b] - north_mean
                    south = ref[j, 1, b] - south_mean
                    for q, part in ((0, north + south), (1, north - south)):
                        for v in range(LEV):
                            row = (q * 8 + ens * 4 + b * 2 + v) * 16 + j
                            left[row : row + 1, :] = part[v : v + 1, :]
        high, low = split_rows(left[...])
        split[0:256, :] = high
        split[256:512, :] = low

    both = jnp.dot(split[...], high_ref[...], preferred_element_type=f32)
    result = both[0:256] + both[256:512]
    result = result + jnp.dot(split[0:256, :], low_ref[...], preferred_element_type=f32)
    for o in range(16):
        block = jnp.concatenate(
            [result[x * 16 : x * 16 + 16, o * 40 : o * 40 + 40] for x in range(16)], axis=1
        )
        out_a[o * 8 : o * 8 + 8, :] = block[0:8]
        out_b[o] = block[8:10]


def forward_fourier(prior, posterior, mean, high, low):
    full = pl.BlockSpec((HALF, 2, 2, LEV, NLON), lambda i: (0, 0, 0, 0, 0))
    return pl.pallas_call(
        forward_kernel,
        grid=(2,),
        out_shape=(
            jax.ShapeDtypeStruct((NG * 8, 640), f32),
            jax.ShapeDtypeStruct((NG, 2, 640), f32),
        ),
        in_specs=[
            full,
            full,
            pl.BlockSpec((40, LEV, NLON), lambda i: (0, 0, 0)),
            pl.BlockSpec((NLON, 640), lambda i: (0, i)),
            pl.BlockSpec((NLON, 640), lambda i: (0, i)),
        ],
        out_specs=(
            pl.BlockSpec((NG * 4, 640), lambda i: (i, 0)),
            pl.BlockSpec((NG // 2, 2, 640), lambda i: (i, 0, 0)),
        ),
        scratch_shapes=[pltpu.VMEM((256, NLON), f32), pltpu.VMEM((512, NLON), bf16)],
        compiler_params=pltpu.CompilerParams(vmem_limit_bytes=BIG),
        name="forward_fourier",
    )(prior, posterior, mean, high, low)


def exchange_kernel(src_a, src_b, dst_a, dst_b, local_sem, send_sem, recv_sem):
    me = lax.axis_index("grid")
    y, z = lax.div(me, NZ), lax.rem(me, NZ)
    barrier = pltpu.get_barrier_semaphore()

    def peer_of(k):
        return lax.rem(y + k // NZ, NY) * NZ + lax.rem(z + k % NZ, NZ)

    def eight(place):
        return pl.ds(pl.multiple_of(place * 8, 8), 8)

    for k in range(1, NG):
        pl.semaphore_signal(barrier, inc=1, device_id={"grid": peer_of(k)}, device_id_type=MESH)
    mine = [
        pltpu.make_async_copy(src_a.at[eight(me), :], dst_a.at[eight(me), :], local_sem.at[0]),
        pltpu.make_async_copy(src_b.at[me], dst_b.at[me], local_sem.at[1]),
    ]
    for copy in mine:
        copy.start()
    pl.semaphore_wait(barrier, NG - 1)
    copies = []
    order = sorted(range(1, NG), key=lambda k: -min(k % NZ, NZ - k % NZ))
    for k in order:
        peer = peer_of(k)
        for part, source, target in (
            (0, src_a.at[eight(peer), :], dst_a.at[eight(me), :]),
            (1, src_b.at[peer], dst_b.at[me]),
        ):
            copy = pltpu.make_async_remote_copy(
                src_ref=source,
                dst_ref=target,
                send_sem=send_sem.at[part, k],
                recv_sem=recv_sem.at[part, k],
                device_id={"grid": peer},
                device_id_type=MESH,
            )
            copy.start()
            copies.append(copy)
    for copy in mine + copies:
        copy.wait()


def exchange(values, collective_id):
    return pl.pallas_call(
        exchange_kernel,
        out_shape=tuple(jax.ShapeDtypeStruct(v.shape, f32) for v in values),
        in_specs=[pl.BlockSpec(memory_space=pltpu.VMEM)] * 2,
        out_specs=(pl.BlockSpec(memory_space=pltpu.VMEM),) * 2,
        scratch_shapes=[
            pltpu.SemaphoreType.DMA((2,)),
            pltpu.SemaphoreType.DMA((2, NG)),
            pltpu.SemaphoreType.DMA((2, NG)),
        ],
        compiler_params=pltpu.CompilerParams(
            collective_id=collective_id, has_side_effects=True, vmem_limit_bytes=BIG
        ),
        name="exchange_%d" % collective_id,
    )(*values)


def analyse_kernel(
    src_a, src_b, weight_ref, place_ref, table_ref, spectral_ref, power_ref, turned, total, pairs
):
    p = pl.program_id(0)

    @pl.when(p == 0)
    def _():
        for g in range(NG):
            two = src_b[g]
            pairs[g * 2 : g * 2 + 2, :] = two
            pairs[64 + g * 2 : 64 + g * 2 + 2, :] = two
        for t in range(2):
            at = t * 128
            turned[t] = src_a[at : at + 128, :].T * weight_ref[:, at : at + 128]
        turned[2] = pairs[...].T * weight_ref[:, 256:384]
        total[...] = jnp.zeros_like(total)

    pair = place_ref[0] * HALF + p
    odd_pair = lax.rem(p, 2)
    lane = lax.broadcasted_iota(jnp.int32, (16, TROWS), 1)
    first_weight = jnp.where(pair == 0, 1.0, 2.0).astype(f32)
    for q in range(2):
        groups = []
        for e in range(2):
            parity = lax.rem(q + odd_pair + 1 - e, 2)
            for part in range(2):
                start = parity * 320 + p * 4 + e * 2 + part
                groups.append(
                    jnp.concatenate(
                        [turned[t, pl.ds(start, 8, stride=40), :] for t in range(3)], axis=1
                    )
                )
        high, low = split_rows(jnp.concatenate(groups, axis=0))
        left = jnp.concatenate(
            [
                jnp.concatenate([high[:, 0:256], high[:, 0:256], high[:, 256:384]], axis=1),
                jnp.concatenate([low[:, 0:256], low[:, 0:256], low[:, 256:384]], axis=1),
            ],
            axis=0,
        )
        both = lax.dot_general(
            left, table_ref[q], (((1,), (1,)), ((), ())), preferred_element_type=f32
        )
        result = both[0:32] + both[32:64]
        in_first = 2 * lane + q < NLAT - pair
        chosen = jnp.where(in_first, result[0:16], result[16:32])
        spectral_ref[q] = chosen
        squares = chosen * chosen
        total[0, :, q * TROWS : (q + 1) * TROWS] += jnp.where(in_first, squares, 0.0) * first_weight
        total[1, :, q * TROWS : (q + 1) * TROWS] += jnp.where(in_first, 0.0, squares) * 2.0

    @pl.when(p == HALF - 1)
    def _():
        for s in range(2):
            merged = total[s, 0:8, :] + total[s, 8:16, :]
            for ens in range(2):
                row = s * 4 + ens * 2
                power_ref[row : row + 2, 0:768] = (
                    merged[ens * 4 : ens * 4 + 2, :] + merged[ens * 4 + 2 : ens * 4 + 4, :]
                )
        power_ref[:, 768:1024] = jnp.zeros((8, 256), f32)


def analyse(arrived, weights, place, table):
    return pl.pallas_call(
        analyse_kernel,
        grid=(HALF,),
        out_shape=(
            jax.ShapeDtypeStruct((2 * HALF, 16, TROWS), f32),
            jax.ShapeDtypeStruct((8, 1024), f32),
        ),
        in_specs=[
            pl.BlockSpec((NG * 8, 640), lambda i: (0, 0)),
            pl.BlockSpec((NG, 2, 640), lambda i: (0, 0, 0)),
            pl.BlockSpec((1, TROWS), lambda i: (0, 0)),
            pl.BlockSpec(memory_space=pltpu.SMEM),
            pl.BlockSpec((2, TROWS, 640), lambda i: (i, 0, 0)),
        ],
        out_specs=(
            pl.BlockSpec((2, 16, TROWS), lambda i: (i, 0, 0)),
            pl.BlockSpec((8, 1024), lambda i: (0, 0)),
        ),
        scratch_shapes=[pltpu.VMEM((3, 640, 128), f32), pltpu.VMEM((2, 16, 2 * TROWS), f32),
            pltpu.VMEM((128, 640), f32),
        ],
        compiler_params=pltpu.CompilerParams(vmem_limit_bytes=BIG),
        name="analyse",
    )(*arrived, weights, place, table)


def power_kernel(src, out, own, at_m, at_y, at_z, s1, r1, s2, r2, s3, r3, s4, r4):
    mem = lax.axis_index("mem")
    grid = lax.axis_index("grid")
    y, z = lax.div(grid, NZ), lax.rem(grid, NZ)
    barrier = pltpu.get_barrier_semaphore()

    def mem_peer(k):
        return {"mem": lax.rem(mem + k, NM)}

    def y_peer(k):
        return {"grid": lax.rem(y + k, NY) * NZ + z}

    def z_peer(k):
        return {"grid": y * NZ + lax.rem(z + k, NZ)}

    for peer, count in ((mem_peer, NM), (y_peer, NY), (z_peer, NZ)):
        for k in range(1, count):
            pl.semaphore_signal(barrier, inc=1, device_id=peer(k), device_id_type=MESH)
    pl.semaphore_wait(barrier, NM + NY + NZ - 3)

    def send(source, target, k, sends, receives, device):
        copy = pltpu.make_async_remote_copy(
            src_ref=source,
            dst_ref=target,
            send_sem=sends.at[k - 1],
            recv_sem=receives.at[k - 1],
            device_id=device,
            device_id_type=MESH,
        )
        copy.start()
        return copy

    def lanes(index):
        return pl.ds(pl.multiple_of(index * 128, 128), 128)

    pending = []
    now = [
        send(src.at[:, lanes(lax.rem(mem + k, NM))], at_m.at[k - 1], k, s1, r1, mem_peer(k))
        for k in range(1, NM)
    ]
    value = src[:, lanes(mem)]
    for k, copy in enumerate(now):
        copy.wait_recv()
        value = value + at_m[k]
    pending += now
    for stage, (peer, count, sends, receives, slots) in enumerate(
        ((y_peer, NY, s2, r2, at_y), (z_peer, NZ, s3, r3, at_z))
    ):
        own[stage] = value
        now = [
            send(own.at[stage], slots.at[k - 1], k, sends, receives, peer(k))
            for k in range(1, count)
        ]
        for k, copy in enumerate(now):
            copy.wait_recv()
            value = value + slots[k]
        pending += now
    own[2] = value
    out[:, lanes(mem)] = value
    now = [
        send(own.at[2], out.at[:, lanes(mem)], k, s4, r4, mem_peer(k)) for k in range(1, NM)
    ]
    for copy in now:
        copy.wait()
    for copy in pending:
        copy.wait_send()


def power_sum(power):
    return pl.pallas_call(
        power_kernel,
        out_shape=jax.ShapeDtypeStruct((8, 1024), f32),
        in_specs=[pl.BlockSpec(memory_space=pltpu.VMEM)],
        out_specs=pl.BlockSpec(memory_space=pltpu.VMEM),
        scratch_shapes=[
            pltpu.VMEM((3, 8, 128), f32),
            pltpu.VMEM((NM - 1, 8, 128), f32),
            pltpu.VMEM((NY - 1, 8, 128), f32),
            pltpu.VMEM((NZ - 1, 8, 128), f32),
        ]
        + [pltpu.SemaphoreType.DMA((n - 1,)) for n in (NM, NM, NY, NY, NZ, NZ, NM, NM)],
        compiler_params=pltpu.CompilerParams(
            collective_id=2, has_side_effects=True, vmem_limit_bytes=BIG
        ),
        name="power_sum",
    )(power)


def synth_kernel(
    power_ref, relax_ref, place_ref, spectral_ref, table_ref, out_a, out_b, ratio, turned
):
    p = pl.program_id(0)

    @pl.when(p == 0)
    def _():
        row = lax.broadcasted_iota(jnp.int32, (TROWS, TROWS), 0)
        column = lax.broadcasted_iota(jnp.int32, (TROWS, TROWS), 1)
        relaxation = jnp.where(
            lax.broadcasted_iota(jnp.int32, (2, TROWS), 0) == 0, relax_ref[0], relax_ref[1]
        )
        place_row = lax.broadcasted_iota(jnp.int32, (2, TROWS), 1)
        odd_row = lax.rem(lax.broadcasted_iota(jnp.int32, (16, TROWS), 0), 2) == 1
        for q in range(2):
            reverse = jnp.where(row + column == 320 - q, 1.0, 0.0).astype(f32)
            part = power_ref[:, q * TROWS : (q + 1) * TROWS]
            flipped = jnp.dot(
                part, reverse, precision=lax.Precision.HIGHEST, preferred_element_type=f32
            )
            power_prior = flipped[0:2] + part[4:6]
            power_post = flipped[2:4] + part[6:8]
            degree = jnp.maximum(2 * place_row + (q - 1), 0).astype(f32)
            samples = MEMBERS * (2.0 * degree + 1.0)
            spread = (power_prior / samples + EPS) / (power_post / samples + EPS)
            value = (1.0 - relaxation) + relaxation * jnp.sqrt(spread)
            back = jnp.dot(
                jnp.concatenate([value] * 4, axis=0),
                reverse,
                precision=lax.Precision.HIGHEST,
                preferred_element_type=f32,
            )
            ratio[q, 0] = jnp.where(odd_row, back[1:2], back[0:1])
            ratio[q, 1] = jnp.where(odd_row, value[1:2], value[0:1])

    pair = place_ref[0] * HALF + p
    odd_pair = lax.rem(p, 2)
    lane = lax.broadcasted_iota(jnp.int32, (16, TROWS), 1)
    for q in range(2):
        in_first = 2 * lane + q < NLAT - pair
        inside = 2 * lane + q <= NLAT
        values = spectral_ref[q]
        rows = jnp.concatenate(
            [
                jnp.where(in_first, values * ratio[q, 0], 0.0),
                jnp.where(inside & ~in_first, values * ratio[q, 1], 0.0),
            ],
            axis=0,
        )
        high, low = split_rows(rows)
        both = jnp.dot(
            jnp.concatenate([high, low], axis=0), table_ref[q], preferred_element_type=f32
        )
        result = both[0:32] + both[32:64]
        a_part = result[:, 0:256] + result[:, 256:512]
        b_part = result[:, 512:640]
        b_part = b_part + pltpu.roll(b_part, 64, 1)
        for e in range(2):
            parity = lax.rem(q + odd_pair + 1 - e, 2)
            for part in range(2):
                at = e * 16 + part * 8 + 4
                start = parity * 160 + p * 4 + e * 2 + part
                where = pl.ds(start, 4, stride=40)
                turned[0, where, :] = a_part[at : at + 4, 0:128]
                turned[1, where, :] = a_part[at : at + 4, 128:256]
                turned[2, where, :] = b_part[at : at + 4]

    @pl.when(p == HALF - 1)
    def _():
        for t in range(2):
            out_a[t * 128 : t * 128 + 128, :] = turned[t].T
        b_rows = turned[2].T
        for g in range(NG):
            out_b[g] = b_rows[g * 2 : g * 2 + 2, :]


def synthesise(power, relaxation, place, spectral, table):
    return pl.pallas_call(
        synth_kernel,
        grid=(HALF,),
        out_shape=(
            jax.ShapeDtypeStruct((NG * 8, TROWS), f32),
            jax.ShapeDtypeStruct((NG, 2, TROWS), f32),
        ),
        in_specs=[
            pl.BlockSpec((8, 1024), lambda i: (0, 0)),
            pl.BlockSpec(memory_space=pltpu.SMEM),
            pl.BlockSpec(memory_space=pltpu.SMEM),
            pl.BlockSpec((2, 16, TROWS), lambda i: (i, 0, 0)),
            pl.BlockSpec((2, TROWS, 640), lambda i: (i, 0, 0)),
        ],
        out_specs=(
            pl.BlockSpec((NG * 8, TROWS), lambda i: (0, 0)),
            pl.BlockSpec((NG, 2, TROWS), lambda i: (0, 0, 0)),
        ),
        scratch_shapes=[
            pltpu.VMEM((2, 2, 16, TROWS), f32),
            pltpu.VMEM((3, TROWS, 128), f32),
        ],
        compiler_params=pltpu.CompilerParams(vmem_limit_bytes=BIG),
        name="synthesise",
    )(power, relaxation, place, spectral, table)


def inverse_kernel(src_a, src_b, mean_ref, high_ref, low_ref, out_ref, split, joined):
    @pl.when(pl.program_id(0) == 0)
    def _():
        for o in range(NG):
            joined[o * 16 : o * 16 + 8, :] = src_a[o * 8 : o * 8 + 8, :]
            joined[o * 16 + 8 : o * 16 + 10, :] = src_b[o]
            joined[o * 16 + 10 : o * 16 + 16, :] = jnp.zeros((6, TROWS), f32)
        for x in range(8):
            row = jnp.concatenate(
                [
                    joined[o * 16 : o * 16 + 16, x * 40 : x * 40 + 40]
                    for o in range(NG)
                ],
                axis=1,
            )
            high, low = split_rows(row)
            split[x * 16 : x * 16 + 16, :] = high
            split[128 + x * 16 : 128 + x * 16 + 16, :] = low

    both = jnp.dot(split[...], high_ref[...], preferred_element_type=f32)
    result = both[0:128] + both[128:256]
    result = result + jnp.dot(split[0:128, :], low_ref[...], preferred_element_type=f32)
    north = result[0:64] + result[64:128]
    south = result[0:64] - result[64:128]
    for h, part in ((0, north), (1, south)):
        for j in range(HALF):
            mean = mean_ref[20 + j * 2 + h]
            for b in range(2):
                for v in range(LEV):
                    row = (b * 2 + v) * 16 + j
                    out_ref[j, h, b, v : v + 1, :] = part[row : row + 1, :] + mean[v : v + 1, :]


def inverse_fourier(returned, mean, high, low):
    width = 640
    return pl.pallas_call(
        inverse_kernel,
        grid=(NLON // width,),
        out_shape=jax.ShapeDtypeStruct((HALF, 2, 2, LEV, NLON), f32),
        in_specs=[
            pl.BlockSpec((NG * 8, TROWS), lambda i: (0, 0)),
            pl.BlockSpec((NG, 2, TROWS), lambda i: (0, 0, 0)),
            pl.BlockSpec((40, LEV, width), lambda i: (0, 0, i)),
            pl.BlockSpec((NLON, width), lambda i: (0, i)),
            pl.BlockSpec((NLON, width), lambda i: (0, i)),
        ],
        out_specs=pl.BlockSpec((HALF, 2, 2, LEV, width), lambda i: (0, 0, 0, 0, i)),
        scratch_shapes=[pltpu.VMEM((256, NLON), bf16), pltpu.VMEM((NG * 16, TROWS), f32)],
        compiler_params=pltpu.CompilerParams(vmem_limit_bytes=BIG),
        name="inverse_fourier",
    )(*returned, mean, high, low)


def lane_order(values):
    grouped = values.reshape(NG, HALF)
    eight = grouped[:, 0:8].reshape(1, 256)
    two = grouped[:, 8:10].reshape(1, 64)
    return jnp.concatenate([eight, two, two], axis=1)


def per_device(prior, posterior, cycle_rows, relaxation):
    forward_high, forward_low, inverse_high, inverse_low = (jnp.asarray(t) for t in trig_tables())
    place = lax.axis_index("grid").astype(jnp.int32)
    place_array = place.reshape(1)
    colatitude = math.pi * (lane_order(cycle_rows).astype(f32) + 0.5) / NLAT
    sines = jnp.sin(colatitude)
    cosines = jnp.cos(colatitude)
    weights = math.pi / NLAT * sines
    pairs = place * HALF + jnp.arange(16, dtype=jnp.int32)
    orders = jnp.clip(jnp.stack([pairs, NLAT - 1 - pairs]), 0, NLAT - 1)
    starts = jnp.take(jnp.asarray(leading_logs()), orders)[:, :, None]
    starts = starts + orders.astype(f32)[:, :, None] * jnp.log(sines)[None]

    mean = member_means(prior, posterior)
    table = legendre_table(starts, cosines, place_array)
    sent = forward_fourier(prior, posterior, mean, forward_high, forward_low)
    arrived = exchange(sent, 1)
    spectral, power = analyse(arrived, weights, place_array, table)
    power = power_sum(power)
    sent_back = synthesise(power, relaxation, place_array, spectral, table)
    returned = exchange(sent_back, 3)
    return inverse_fourier(returned, mean, inverse_high, inverse_low)


def solution(mesh):
    return jax.shard_map(
        per_device,
        mesh=mesh,
        in_specs=(P("grid", None, "mem", None, None), P("grid", None, "mem", None, None), P(), P()),
        out_specs=P("grid", None, "mem", None, None),
        check_vma=False,
    )
```

```python
import functools
import math

import jax
import jax.numpy as jnp
import ml_dtypes
import numpy as np
from jax import lax
from jax.experimental import pallas as pl
from jax.experimental.pallas import tpu as pltpu
from jax.sharding import PartitionSpec as P

MESH = pl.DeviceIdType.MESH
NLAT = 640
LEV = 2
NLON = 1280
NPAIR = 320
MEMBERS = 16
NG = 32
NM = 8
NY = 4
NZ = 8
HALF = 10
EPS = 1e-06
ROWS = 672
TROWS = 384
PITCH = 17
SIDE = 5720
BIG = 60 * 1024 * 1024

f32 = jnp.float32
bf16 = jnp.bfloat16


def split_table(table):
    hi = table.astype(np.float32).astype(ml_dtypes.bfloat16)
    lo = (table - hi.astype(np.float64)).astype(np.float32).astype(ml_dtypes.bfloat16)
    return hi, lo


@functools.lru_cache(maxsize=None)
def trig_tables():
    owner = np.arange(NG)[:, None, None]
    pair = np.arange(HALF)[None, :, None]
    segment = np.arange(2)[None, None, :]
    first = owner * HALF + pair
    order = np.where(segment == 0, first, NLAT - 1 - first).reshape(-1)
    phase = (np.arange(NLON)[:, None] * order[None, :]) % NLON
    angle = 2.0 * np.pi / NLON * phase
    table = np.stack([np.cos(angle), -np.sin(angle)], axis=-1).reshape(NLON, NLON)
    weight = np.repeat(np.where(order == 0, 1.0, 2.0) / NLON, 2)
    return split_table(table) + split_table((table * weight[None, :]).T)


@functools.lru_cache(maxsize=None)
def leading_logs():
    i = np.arange(1, NLAT + 1, dtype=np.float64)
    total = np.concatenate([[0.0], np.cumsum(np.log((2 * i - 1) / (2 * i)))])[:NLAT]
    m = np.arange(NLAT, dtype=np.float64)
    leading = 0.5 * (np.log((2 * m + 1) / 2) + total)
    pair = np.arange(NG)[:, None] * HALF + np.arange(16)[None, :]
    orders = np.clip(np.stack([pair, NLAT - 1 - pair], axis=1), 0, NLAT - 1)
    return np.ascontiguousarray(
        np.broadcast_to(leading[orders][..., None], (NG, 2, 16, 128)).astype(np.float32)
    )


def split_rows(values):
    high = values.astype(bf16)
    low = (values - high.astype(f32)).astype(bf16)
    return high, low


def place_of(side, index):
    return side * SIDE + index * PITCH


def build_legendre(place, lead_ref, lats_ref, table_ref, rows):
    zero = jnp.zeros((16, TROWS), f32)
    for i in range(641, ROWS):
        for t in range(3):
            rows[t, pl.ds(place_of(i % 2, i // 2), 16), :] = zero[:, 0:128]
    sub = lax.broadcasted_iota(jnp.int32, (16, 128), 0)
    step = lax.rem(lax.broadcasted_iota(jnp.int32, (16, 128), 1), 8)
    cosine = jnp.broadcast_to(lats_ref[0:1, :], (16, TROWS))
    log_sine = jnp.broadcast_to(lats_ref[2:3, :], (16, TROWS))
    valid = sub < HALF
    pair = jnp.where(valid, place * HALF + sub, 4 * NLAT)

    def chain(segment, first_block, order):
        def block(b, state):
            current, earlier, scale_log = state
            degree = (b * 8 + step).astype(f32)
            m = order.astype(f32)
            inside = valid & (b * 8 + step > order)
            square = degree * degree
            difference = jnp.where(inside, square - m * m, 1.0)
            low = degree - 1.0
            low_square = low * low
            lead = (4.0 * square - 1.0) / difference
            trail = jnp.maximum(low_square - m * m, 0.0) / jnp.maximum(4.0 * low_square - 1.0, 1.0)
            a = jnp.where(inside, jnp.sqrt(jnp.maximum(lead, 0.0)), 0.0)
            c = jnp.where(inside, a * jnp.sqrt(trail), 0.0)
            scale = jnp.exp(scale_log)
            for k in range(8):
                ak = jnp.broadcast_to(a[:, k : k + 1], (16, TROWS))
                ck = jnp.broadcast_to(c[:, k : k + 1], (16, TROWS))
                following = (ak * cosine) * current - ck * earlier
                begin = order == b * 8 + k
                following = jnp.where(jnp.concatenate([begin] * 3, axis=1), 1.0, following)
                earlier = current
                current = following
                entry = current * scale
                degree_now = b * 8 + k
                side = (k + 1) % 2
                if segment == 0:
                    offset = place_of(side, (NLAT - 1 - k - side) // 2 - 4 * b)
                else:
                    offset = place_of(side, 4 * b + (k + 1 - side) // 2)
                    second = degree_now >= NLAT - 1 - pair
                for t in range(3):
                    tile = entry[:, t * 128 : t * 128 + 128]
                    if segment == 1:
                        tile = jnp.where(second, tile, rows[t, pl.ds(offset, 16), :])
                    rows[t, pl.ds(offset, 16), :] = tile
            large = jnp.abs(current) > 1e10
            current = jnp.where(large, current * 1e-20, current)
            earlier = jnp.where(large, earlier * 1e-20, earlier)
            scale_log = jnp.where(large, scale_log + 20.0 * math.log(10.0), scale_log)
            return current, earlier, scale_log

        leading = jnp.concatenate([lead_ref[segment]] * 3, axis=1)
        wide = jnp.concatenate([order.astype(f32)] * 3, axis=1)
        lax.fori_loop(first_block, NLAT // 8, block, (zero, zero, leading + wide * log_sine))

    chain(0, lax.div(place * HALF, 8), pair)
    chain(1, lax.div(NLAT - HALF - place * HALF, 8), NLAT - 1 - pair)

    right = lax.broadcasted_iota(jnp.int32, (16, 128), 1) < 64
    blank = jnp.zeros((TROWS - ROWS // 2, 640), bf16)
    for p in range(HALF):
        for q in range(2):

            def convert(t, carry):
                out = pl.ds(pl.multiple_of(t * 16, 16), 16)
                for tile in range(3):
                    values = rows[tile, pl.ds(q * SIDE + t * 16 * PITCH + p, 16, stride=PITCH), :]
                    high = values.astype(bf16)
                    low = values - high.astype(f32)
                    if tile < 2:
                        at = tile * 128
                        table_ref[p * 2 + q, out, at : at + 128] = high
                        table_ref[p * 2 + q, out, at + 256 : at + 384] = low.astype(bf16)
                    else:
                        table_ref[p * 2 + q, out, 512:640] = jnp.where(right, values, low).astype(bf16)
                return carry

            lax.fori_loop(0, ROWS // 32, convert, 0, unroll=3)
            table_ref[p * 2 + q, ROWS // 2 : TROWS, :] = blank


def spectral_kernel(
    prior_ref,
    post_ref,
    lats_ref,
    relax_ref,
    lead_hbm,
    high_hbm,
    low_hbm,
    mean_ref,
    back_a,
    back_b,
    sums,
    arrived,
    piece,
    lead,
    trig_high,
    trig_low,
    left,
    split,
    out_a,
    out_b,
    in_a,
    in_b,
    rows,
    table,
    pairs,
    turned,
    total,
    spectral,
    power,
    summed,
    own,
    at_m,
    at_y,
    at_z,
    ratio,
    merged,
    ret_a,
    ret_b,
    local_sem,
    s_rs,
    r_rs,
    s_ag,
    r_ag,
    s_ex,
    r_ex,
    s_p1,
    r_p1,
    s_p2,
    r_p2,
    s_p3,
    r_p3,
    s_p4,
    r_p4,
    s_re,
    r_re,
):
    mem = lax.axis_index("mem")
    me = lax.axis_index("grid")
    y, z = lax.div(me, NZ), lax.rem(me, NZ)
    barrier = pltpu.get_barrier_semaphore()

    def peer_of(k):
        return lax.rem(y + k // NZ, NY) * NZ + lax.rem(z + k % NZ, NZ)

    def eight(place):
        return pl.ds(pl.multiple_of(place * 8, 8), 8)

    def mem_peer(k):
        return {"mem": lax.rem(mem + k, NM)}

    def send(source, target, send_sem, recv_sem, device):
        copy = pltpu.make_async_remote_copy(
            src_ref=source,
            dst_ref=target,
            send_sem=send_sem,
            recv_sem=recv_sem,
            device_id=device,
            device_id_type=MESH,
        )
        copy.start()
        return copy

    for k in range(1, NM):
        pl.semaphore_signal(barrier, inc=1, device_id=mem_peer(k), device_id_type=MESH)
    for k in range(1, NG):
        pl.semaphore_signal(barrier, inc=1, device_id={"grid": peer_of(k)}, device_id_type=MESH)
    loads = [
        pltpu.make_async_copy(high_hbm, trig_high, local_sem.at[0]),
        pltpu.make_async_copy(low_hbm, trig_low, local_sem.at[1]),
        pltpu.make_async_copy(lead_hbm.at[me], lead, local_sem.at[2]),
    ]
    for copy in loads:
        copy.start()

    for ens, ref in ((0, prior_ref), (1, post_ref)):
        for j in range(HALF):
            for h in range(2):
                sums[ens * 20 + j * 2 + h] = ref[j, h, 0] + ref[j, h, 1]
    left[...] = jnp.zeros_like(left)
    pl.semaphore_wait(barrier, NM + NG - 2)
    pending = []
    now = []
    for k in range(1, NM):
        peer = lax.rem(mem + k, NM)
        now.append(
            send(
                sums.at[pl.ds(peer * 5, 5)],
                arrived.at[k - 1],
                s_rs.at[k - 1],
                r_rs.at[k - 1],
                mem_peer(k),
            )
        )
    value = sums[pl.ds(mem * 5, 5)]
    for k, copy in enumerate(now):
        copy.wait_recv()
        value = value + arrived[k]
    pending += now
    piece[...] = value * (1.0 / MEMBERS)
    mean_ref[pl.ds(mem * 5, 5)] = piece[...]
    now = [
        send(piece, mean_ref.at[pl.ds(mem * 5, 5)], s_ag.at[k - 1], r_ag.at[k - 1], mem_peer(k))
        for k in range(1, NM)
    ]
    for copy in now:
        copy.wait_recv()
    pending += now

    for ens, ref in ((0, prior_ref), (1, post_ref)):
        for j in range(HALF):
            north_mean = mean_ref[ens * 20 + j * 2]
            south_mean = mean_ref[ens * 20 + j * 2 + 1]
            for b in range(2):
                north = ref[j, 0, b] - north_mean
                south = ref[j, 1, b] - south_mean
                for q, part in ((0, north + south), (1, north - south)):
                    for v in range(LEV):
                        row = (q * 8 + ens * 4 + b * 2 + v) * 16 + j
                        left[row : row + 1, :] = part[v : v + 1, :]
    high, low = split_rows(left[...])
    split[0:256, :] = high
    split[256:512, :] = low
    for copy in loads:
        copy.wait()
    own_half = lax.div(y, 2)
    exchanged = []
    for step in range(2):
        half = own_half if step == 0 else 1 - own_half
        columns = pl.ds(pl.multiple_of(half * 640, 128), 640)
        both = jnp.dot(split[...], trig_high[:, columns], preferred_element_type=f32)
        result = both[0:256] + both[256:512]
        result = result + jnp.dot(
            split[0:256, :], trig_low[:, columns], preferred_element_type=f32
        )
        for o in range(16):
            block = jnp.concatenate(
                [result[x * 16 : x * 16 + 16, o * 40 : o * 40 + 40] for x in range(16)], axis=1
            )
            place = half * 16 + o
            out_a[eight(place), :] = block[0:8]
            out_b[place] = block[8:10]
        for j in range(2):
            if step == 0:
                far_y = y if j == 0 else y + 1 - 2 * lax.rem(y, 2)
            else:
                far_y = 2 * half + lax.rem(y + j, 2)
            for dz in (4, 3, 5, 2, 6, 1, 7, 0):
                if step == 0 and j == 0 and dz == 0:
                    continue
                peer = far_y * NZ + lax.rem(z + dz, NZ)
                k = (step * 2 + j) * 8 + dz
                exchanged.append(
                    send(
                        out_a.at[eight(peer), :],
                        in_a.at[eight(me), :],
                        s_ex.at[0, k],
                        r_ex.at[0, k],
                        {"grid": peer},
                    )
                )
                exchanged.append(
                    send(out_b.at[peer], in_b.at[me], s_ex.at[1, k], r_ex.at[1, k], {"grid": peer})
                )

    build_legendre(me, lead, lats_ref, table, rows)

    in_a[eight(me), :] = out_a[eight(me), :]
    in_b[me] = out_b[me]
    for copy in exchanged:
        copy.wait_recv()
    pending += exchanged
    for g in range(NG):
        two = in_b[g]
        pairs[g * 2 : g * 2 + 2, :] = two
        pairs[64 + g * 2 : 64 + g * 2 + 2, :] = two
    for t in range(2):
        at = t * 128
        turned[t] = in_a[at : at + 128, :].T * lats_ref[1:2, at : at + 128]
    turned[2] = pairs[...].T * lats_ref[1:2, 256:384]
    total[...] = jnp.zeros_like(total)
    lane = lax.broadcasted_iota(jnp.int32, (16, TROWS), 1)

    def analyse_pair(p, odd):
        pair = me * HALF + p
        first_weight = jnp.where(pair == 0, 1.0, 2.0).astype(f32)
        for q in range(2):
            groups = []
            for e in range(2):
                parity = (q + odd + 1 - e) % 2
                for part in range(2):
                    start = parity * 320 + p * 4 + e * 2 + part
                    groups.append(
                        jnp.concatenate(
                            [turned[t, pl.ds(start, 8, stride=40), :] for t in range(3)], axis=1
                        )
                    )
            high, low = split_rows(jnp.concatenate(groups, axis=0))
            operand = jnp.concatenate(
                [
                    jnp.concatenate([high[:, 0:256], high[:, 0:256], high[:, 256:384]], axis=1),
                    jnp.concatenate([low[:, 0:256], low[:, 0:256], low[:, 256:384]], axis=1),
                ],
                axis=0,
            )
            both = lax.dot_general(
                operand,
                table[p * 2 + q],
                (((1,), (1,)), ((), ())),
                preferred_element_type=f32,
            )
            result = both[0:32] + both[32:64]
            in_first = 2 * lane + q < NLAT - pair
            chosen = jnp.where(in_first, result[0:16], result[16:32])
            spectral[p * 2 + q] = chosen
            squares = chosen * chosen
            where = slice(q * TROWS, (q + 1) * TROWS)
            total[0, :, where] += jnp.where(in_first, squares, 0.0) * first_weight
            total[1, :, where] += jnp.where(in_first, 0.0, squares) * 2.0

    def analyse_two(i, carry):
        analyse_pair(2 * i, 0)
        analyse_pair(2 * i + 1, 1)
        return carry

    lax.fori_loop(0, HALF // 2, analyse_two, 0)
    for s in range(2):
        both = total[s, 0:8, :] + total[s, 8:16, :]
        for ens in range(2):
            row = s * 4 + ens * 2
            power[row : row + 2, 0:768] = both[ens * 4 : ens * 4 + 2] + both[ens * 4 + 2 : ens * 4 + 4]
    power[:, 768:1024] = jnp.zeros((8, 256), f32)

    def lanes(index):
        return pl.ds(pl.multiple_of(index * 128, 128), 128)

    now = [
        send(
            power.at[:, lanes(lax.rem(mem + k, NM))],
            at_m.at[k - 1],
            s_p1.at[k - 1],
            r_p1.at[k - 1],
            mem_peer(k),
        )
        for k in range(1, NM)
    ]
    value = power[:, lanes(mem)]
    for k, copy in enumerate(now):
        copy.wait_recv()
        value = value + at_m[k]
    pending += now

    def y_peer(k):
        return {"grid": lax.rem(y + k, NY) * NZ + z}

    def z_peer(k):
        return {"grid": y * NZ + lax.rem(z + k, NZ)}

    for stage, (peer, count, sends, receives, slots) in enumerate(
        ((y_peer, NY, s_p2, r_p2, at_y), (z_peer, NZ, s_p3, r_p3, at_z))
    ):
        own[stage] = value
        now = [
            send(own.at[stage], slots.at[k - 1], sends.at[k - 1], receives.at[k - 1], peer(k))
            for k in range(1, count)
        ]
        for k, copy in enumerate(now):
            copy.wait_recv()
            value = value + slots[k]
        pending += now
    own[2] = value
    summed[:, lanes(mem)] = value
    now = [
        send(own.at[2], summed.at[:, lanes(mem)], s_p4.at[k - 1], r_p4.at[k - 1], mem_peer(k))
        for k in range(1, NM)
    ]
    for copy in now:
        copy.wait_recv()
    pending += now

    row = lax.broadcasted_iota(jnp.int32, (TROWS, TROWS), 0)
    column = lax.broadcasted_iota(jnp.int32, (TROWS, TROWS), 1)
    relaxation = jnp.where(
        lax.broadcasted_iota(jnp.int32, (2, TROWS), 0) == 0, relax_ref[0], relax_ref[1]
    )
    place_row = lax.broadcasted_iota(jnp.int32, (2, TROWS), 1)
    odd_row = lax.rem(lax.broadcasted_iota(jnp.int32, (16, TROWS), 0), 2) == 1
    for q in range(2):
        reverse = jnp.where(row + column == 320 - q, 1.0, 0.0).astype(f32)
        part = summed[:, q * TROWS : (q + 1) * TROWS]
        flipped = jnp.dot(
            part, reverse, precision=lax.Precision.HIGHEST, preferred_element_type=f32
        )
        power_prior = flipped[0:2] + part[4:6]
        power_post = flipped[2:4] + part[6:8]
        degree = jnp.maximum(2 * place_row + (q - 1), 0).astype(f32)
        samples = MEMBERS * (2.0 * degree + 1.0)
        spread = (power_prior / samples + EPS) / (power_post / samples + EPS)
        value = (1.0 - relaxation) + relaxation * jnp.sqrt(spread)
        back = jnp.dot(
            jnp.concatenate([value] * 4, axis=0),
            reverse,
            precision=lax.Precision.HIGHEST,
            preferred_element_type=f32,
        )
        ratio[q, 0] = jnp.where(odd_row, back[1:2], back[0:1])
        ratio[q, 1] = jnp.where(odd_row, value[1:2], value[0:1])

    def synth_pair(p, odd):
        pair = me * HALF + p
        for q in range(2):
            in_first = 2 * lane + q < NLAT - pair
            inside = 2 * lane + q <= NLAT
            values = spectral[p * 2 + q]
            high, low = split_rows(
                jnp.concatenate(
                    [
                        jnp.where(in_first, values * ratio[q, 0], 0.0),
                        jnp.where(inside & ~in_first, values * ratio[q, 1], 0.0),
                    ],
                    axis=0,
                )
            )
            both = jnp.dot(
                jnp.concatenate([high, low], axis=0),
                table[p * 2 + q],
                preferred_element_type=f32,
            )
            result = both[0:32] + both[32:64]
            a_part = result[:, 0:256] + result[:, 256:512]
            b_part = result[:, 512:640]
            b_part = b_part + pltpu.roll(b_part, 64, 1)
            for e in range(2):
                parity = (q + odd + 1 - e) % 2
                for part in range(2):
                    at = e * 16 + part * 8 + 4
                    start = parity * 160 + p * 4 + e * 2 + part
                    where = pl.ds(start, 4, stride=40)
                    merged[0, where, :] = a_part[at : at + 4, 0:128]
                    merged[1, where, :] = a_part[at : at + 4, 128:256]
                    merged[2, where, :] = b_part[at : at + 4]

    def synth_two(i, carry):
        synth_pair(2 * i, 0)
        synth_pair(2 * i + 1, 1)
        return carry

    merged[:, 320:384, :] = jnp.zeros((3, 64, 128), f32)
    lax.fori_loop(0, HALF // 2, synth_two, 0)
    for t in range(2):
        ret_a[t * 128 : t * 128 + 128, :] = merged[t].T
    b_rows = merged[2].T
    for g in range(NG):
        ret_b[g] = b_rows[g * 2 : g * 2 + 2, :]

    now = []
    for k in sorted(range(1, NG), key=lambda k: -min(k % NZ, NZ - k % NZ)):
        peer = peer_of(k)
        now.append(
            send(
                ret_a.at[eight(peer), :],
                back_a.at[eight(me), :],
                s_re.at[0, k],
                r_re.at[0, k],
                {"grid": peer},
            )
        )
        now.append(
            send(ret_b.at[peer], back_b.at[me], s_re.at[1, k], r_re.at[1, k], {"grid": peer})
        )
    back_a[eight(me), :] = ret_a[eight(me), :]
    back_b[me] = ret_b[me]
    for copy in now:
        copy.wait()
    for copy in pending:
        copy.wait_send()


def spectral(prior, posterior, lats, relaxation, lead, high, low):
    vmem = pl.BlockSpec(memory_space=pltpu.VMEM)
    hbm = pl.BlockSpec(memory_space=pl.ANY)
    return pl.pallas_call(
        spectral_kernel,
        out_shape=(
            jax.ShapeDtypeStruct((40, LEV, NLON), f32),
            jax.ShapeDtypeStruct((NG * 8, TROWS), f32),
            jax.ShapeDtypeStruct((NG, 2, TROWS), f32),
        ),
        in_specs=[vmem, vmem, vmem, pl.BlockSpec(memory_space=pltpu.SMEM), hbm, hbm, hbm],
        out_specs=(vmem, vmem, vmem),
        scratch_shapes=[
            pltpu.VMEM((40, LEV, NLON), f32),
            pltpu.VMEM((NM - 1, 5, LEV, NLON), f32),
            pltpu.VMEM((5, LEV, NLON), f32),
            pltpu.VMEM((2, 16, 128), f32),
            pltpu.VMEM((NLON, NLON), bf16),
            pltpu.VMEM((NLON, NLON), bf16),
            pltpu.VMEM((256, NLON), f32),
            pltpu.VMEM((512, NLON), bf16),
            pltpu.VMEM((NG * 8, 640), f32),
            pltpu.VMEM((NG, 2, 640), f32),
            pltpu.VMEM((NG * 8, 640), f32),
            pltpu.VMEM((NG, 2, 640), f32),
            pltpu.VMEM((3, 2 * SIDE, 128), f32),
            pltpu.VMEM((2 * HALF, TROWS, 640), bf16),
            pltpu.VMEM((128, 640), f32),
            pltpu.VMEM((3, 640, 128), f32),
            pltpu.VMEM((2, 16, 2 * TROWS), f32),
            pltpu.VMEM((2 * HALF, 16, TROWS), f32),
            pltpu.VMEM((8, 1024), f32),
            pltpu.VMEM((8, 1024), f32),
            pltpu.VMEM((3, 8, 128), f32),
            pltpu.VMEM((NM - 1, 8, 128), f32),
            pltpu.VMEM((NY - 1, 8, 128), f32),
            pltpu.VMEM((NZ - 1, 8, 128), f32),
            pltpu.VMEM((2, 2, 16, TROWS), f32),
            pltpu.VMEM((3, TROWS, 128), f32),
            pltpu.VMEM((NG * 8, TROWS), f32),
            pltpu.VMEM((NG, 2, TROWS), f32),
            pltpu.SemaphoreType.DMA((3,)),
        ]
        + [pltpu.SemaphoreType.DMA((NM - 1,)) for _ in range(4)]
        + [pltpu.SemaphoreType.DMA((2, NG)) for _ in range(2)]
        + [pltpu.SemaphoreType.DMA((n - 1,)) for n in (NM, NM, NY, NY, NZ, NZ, NM, NM)]
        + [pltpu.SemaphoreType.DMA((2, NG)) for _ in range(2)],
        compiler_params=pltpu.CompilerParams(
            collective_id=0, has_side_effects=True, vmem_limit_bytes=BIG
        ),
        name="spectral",
    )(prior, posterior, lats, relaxation, lead, high, low)


def inverse_kernel(src_a, src_b, mean_ref, high_ref, low_ref, out_ref, split, joined):
    @pl.when(pl.program_id(0) == 0)
    def _():
        for o in range(NG):
            joined[o * 16 : o * 16 + 8, :] = src_a[o * 8 : o * 8 + 8, :]
            joined[o * 16 + 8 : o * 16 + 10, :] = src_b[o]
            joined[o * 16 + 10 : o * 16 + 16, :] = jnp.zeros((6, TROWS), f32)
        for x in range(8):
            row = jnp.concatenate(
                [
                    joined[o * 16 : o * 16 + 16, x * 40 : x * 40 + 40]
                    for o in range(NG)
                ],
                axis=1,
            )
            high, low = split_rows(row)
            split[x * 16 : x * 16 + 16, :] = high
            split[128 + x * 16 : 128 + x * 16 + 16, :] = low

    both = jnp.dot(split[...], high_ref[...], preferred_element_type=f32)
    result = both[0:128] + both[128:256]
    result = result + jnp.dot(split[0:128, :], low_ref[...], preferred_element_type=f32)
    north = result[0:64] + result[64:128]
    south = result[0:64] - result[64:128]
    for h, part in ((0, north), (1, south)):
        for j in range(HALF):
            mean = mean_ref[20 + j * 2 + h]
            for b in range(2):
                for v in range(LEV):
                    row = (b * 2 + v) * 16 + j
                    out_ref[j, h, b, v : v + 1, :] = part[row : row + 1, :] + mean[v : v + 1, :]


def inverse_fourier(returned, mean, high, low):
    width = 640
    return pl.pallas_call(
        inverse_kernel,
        grid=(NLON // width,),
        out_shape=jax.ShapeDtypeStruct((HALF, 2, 2, LEV, NLON), f32),
        in_specs=[
            pl.BlockSpec((NG * 8, TROWS), lambda i: (0, 0)),
            pl.BlockSpec((NG, 2, TROWS), lambda i: (0, 0, 0)),
            pl.BlockSpec((40, LEV, width), lambda i: (0, 0, i)),
            pl.BlockSpec((NLON, width), lambda i: (0, i)),
            pl.BlockSpec((NLON, width), lambda i: (0, i)),
        ],
        out_specs=pl.BlockSpec((HALF, 2, 2, LEV, width), lambda i: (0, 0, 0, 0, i)),
        scratch_shapes=[pltpu.VMEM((256, NLON), bf16), pltpu.VMEM((NG * 16, TROWS), f32)],
        compiler_params=pltpu.CompilerParams(vmem_limit_bytes=BIG),
        name="inverse_fourier",
    )(*returned, mean, high, low)


def lane_order():
    grouped = np.arange(NPAIR).reshape(NG, HALF)
    two = grouped[:, 8:10].reshape(-1)
    return np.concatenate([grouped[:, 0:8].reshape(-1), two, two]).astype(np.int32)


def per_device(prior, posterior, cycle_rows, relaxation):
    forward_high, forward_low, inverse_high, inverse_low = (jnp.asarray(t) for t in trig_tables())
    rows = jnp.take(cycle_rows, jnp.asarray(lane_order()))
    colatitude = math.pi * (rows.astype(f32) + 0.5) / NLAT
    sines = jnp.sin(colatitude)
    lats = jnp.stack([jnp.cos(colatitude), math.pi / NLAT * sines, jnp.log(sines)])
    mean, back_a, back_b = spectral(
        prior, posterior, lats, relaxation, jnp.asarray(leading_logs()), forward_high, forward_low
    )
    return inverse_fourier((back_a, back_b), mean, inverse_high, inverse_low)


def solution(mesh):
    return jax.shard_map(
        per_device,
        mesh=mesh,
        in_specs=(P("grid", None, "mem", None, None), P("grid", None, "mem", None, None), P(), P()),
        out_specs=P("grid", None, "mem", None, None),
        check_vma=False,
    )
```

```python
import functools
import math

import jax
import jax.numpy as jnp
import ml_dtypes
import numpy as np
from jax import lax
from jax.experimental import pallas as pl
from jax.experimental.pallas import tpu as pltpu
from jax.sharding import PartitionSpec as P

MESH = pl.DeviceIdType.MESH
NLAT = 640
LEV = 2
NLON = 1280
NPAIR = 320
MEMBERS = 16
NG = 32
NM = 8
NY = 4
NZ = 8
HALF = 10
EPS = 1e-06
ROWS = 672
TROWS = 384
PITCH = 17
EARLY = 32
SIDE = 5720
BIG = 60 * 1024 * 1024

f32 = jnp.float32
bf16 = jnp.bfloat16


def split_table(table):
    hi = table.astype(np.float32).astype(ml_dtypes.bfloat16)
    lo = (table - hi.astype(np.float64)).astype(np.float32).astype(ml_dtypes.bfloat16)
    return hi, lo


@functools.lru_cache(maxsize=None)
def trig_tables():
    owner = np.arange(NG)[:, None, None]
    pair = np.arange(HALF)[None, :, None]
    segment = np.arange(2)[None, None, :]
    first = owner * HALF + pair
    order = np.where(segment == 0, first, NLAT - 1 - first).reshape(-1)
    phase = (np.arange(NLON)[:, None] * order[None, :]) % NLON
    angle = 2.0 * np.pi / NLON * phase
    table = np.stack([np.cos(angle), -np.sin(angle)], axis=-1).reshape(NLON, NLON)
    weight = np.repeat(np.where(order == 0, 1.0, 2.0) / NLON, 2)
    return split_table(table) + split_table((table * weight[None, :]).T)


@functools.lru_cache(maxsize=None)
def leading_logs():
    i = np.arange(1, NLAT + 1, dtype=np.float64)
    total = np.concatenate([[0.0], np.cumsum(np.log((2 * i - 1) / (2 * i)))])[:NLAT]
    m = np.arange(NLAT, dtype=np.float64)
    leading = 0.5 * (np.log((2 * m + 1) / 2) + total)
    pair = np.arange(NG)[:, None] * HALF + np.arange(16)[None, :]
    orders = np.clip(np.stack([pair, NLAT - 1 - pair], axis=1), 0, NLAT - 1)
    return np.ascontiguousarray(
        np.broadcast_to(leading[orders][..., None], (NG, 2, 16, 128)).astype(np.float32)
    )


def split_rows(values):
    high = values.astype(bf16)
    low = (values - high.astype(f32)).astype(bf16)
    return high, low


def place_of(side, index):
    return side * SIDE + index * PITCH


def legendre_parts(place, lead_ref, lats_ref, table_ref, rows, early):
    zero = jnp.zeros((16, TROWS), f32)
    sub = lax.broadcasted_iota(jnp.int32, (16, 128), 0)
    step = lax.rem(lax.broadcasted_iota(jnp.int32, (16, 128), 1), 8)
    cosine = jnp.broadcast_to(lats_ref[0:1, :], (16, TROWS))
    log_sine = jnp.broadcast_to(lats_ref[2:3, :], (16, TROWS))
    valid = sub < HALF
    pair = jnp.where(valid, place * HALF + sub, 4 * NLAT)

    def chain(segment, first_block, last_block, order, state=None):
        def block(b, state):
            current, earlier, scale_log = state
            degree = (b * 8 + step).astype(f32)
            m = order.astype(f32)
            inside = valid & (b * 8 + step > order)
            square = degree * degree
            difference = jnp.where(inside, square - m * m, 1.0)
            low = degree - 1.0
            low_square = low * low
            lead = (4.0 * square - 1.0) / difference
            trail = jnp.maximum(low_square - m * m, 0.0) / jnp.maximum(4.0 * low_square - 1.0, 1.0)
            a = jnp.where(inside, jnp.sqrt(jnp.maximum(lead, 0.0)), 0.0)
            c = jnp.where(inside, a * jnp.sqrt(trail), 0.0)
            scale = jnp.exp(scale_log)
            for k in range(8):
                ak = jnp.broadcast_to(a[:, k : k + 1], (16, TROWS))
                ck = jnp.broadcast_to(c[:, k : k + 1], (16, TROWS))
                following = (ak * cosine) * current - ck * earlier
                begin = order == b * 8 + k
                following = jnp.where(jnp.concatenate([begin] * 3, axis=1), 1.0, following)
                earlier = current
                current = following
                entry = current * scale
                degree_now = b * 8 + k
                side = (k + 1) % 2
                if segment == 0:
                    offset = place_of(side, (NLAT - 1 - k - side) // 2 - 4 * b)
                else:
                    offset = place_of(side, 4 * b + (k + 1 - side) // 2)
                    second = degree_now >= NLAT - 1 - pair
                for t in range(3):
                    tile = entry[:, t * 128 : t * 128 + 128]
                    if segment == 1:
                        tile = jnp.where(second, tile, rows[t, pl.ds(offset, 16), :])
                    rows[t, pl.ds(offset, 16), :] = tile
            large = jnp.abs(current) > 1e10
            current = jnp.where(large, current * 1e-20, current)
            earlier = jnp.where(large, earlier * 1e-20, earlier)
            scale_log = jnp.where(large, scale_log + 20.0 * math.log(10.0), scale_log)
            return current, earlier, scale_log

        leading = jnp.concatenate([lead_ref[segment]] * 3, axis=1)
        wide = jnp.concatenate([order.astype(f32)] * 3, axis=1)
        if state is None:
            state = (zero, zero, leading + wide * log_sine)
        return lax.fori_loop(first_block, last_block, block, state)

    begin_block = lax.div(place * HALF, 8)
    middle = jnp.minimum(begin_block + early, NLAT // 8)

    def start():
        for i in range(641, ROWS):
            for t in range(3):
                rows[t, pl.ds(place_of(i % 2, i // 2), 16), :] = zero[:, 0:128]
        return chain(0, begin_block, middle, pair)

    def finish(state):
        chain(0, middle, NLAT // 8, pair, state)
        chain(1, lax.div(NLAT - HALF - place * HALF, 8), NLAT // 8, NLAT - 1 - pair)

        right = lax.broadcasted_iota(jnp.int32, (16, 128), 1) < 64
        blank = jnp.zeros((TROWS - ROWS // 2, 640), bf16)
        for p in range(HALF):
            for q in range(2):

                def convert(t, carry):
                    out = pl.ds(pl.multiple_of(t * 16, 16), 16)
                    for tile in range(3):
                        values = rows[tile, pl.ds(q * SIDE + t * 16 * PITCH + p, 16, stride=PITCH), :]
                        high = values.astype(bf16)
                        low = values - high.astype(f32)
                        if tile < 2:
                            at = tile * 128
                            table_ref[p * 2 + q, out, at : at + 128] = high
                            table_ref[p * 2 + q, out, at + 256 : at + 384] = low.astype(bf16)
                        else:
                            table_ref[p * 2 + q, out, 512:640] = jnp.where(right, values, low).astype(bf16)
                    return carry

                lax.fori_loop(0, ROWS // 32, convert, 0, unroll=3)
                table_ref[p * 2 + q, ROWS // 2 : TROWS, :] = blank

    return start, finish


def spectral_kernel(
    prior_ref,
    post_ref,
    natural_ref,
    relax_ref,
    lead_hbm,
    high_hbm,
    low_hbm,
    mean_ref,
    back_a,
    back_b,
    sums,
    arrived,
    piece,
    lead,
    trig_high,
    trig_low,
    left,
    split,
    lats_ref,
    out_a,
    out_b,
    in_a,
    in_b,
    rows,
    table,
    pairs,
    turned,
    total,
    spectral,
    power,
    summed,
    own,
    at_m,
    at_g,
    ratio,
    merged,
    ret_a,
    ret_b,
    local_sem,
    s_rs,
    r_rs,
    s_ag,
    r_ag,
    s_ex,
    r_ex,
    s_p1,
    r_p1,
    s_p2,
    r_p2,
    s_p4,
    r_p4,
    s_re,
    r_re,
):
    mem = lax.axis_index("mem")
    me = lax.axis_index("grid")
    y, z = lax.div(me, NZ), lax.rem(me, NZ)
    barrier = pltpu.get_barrier_semaphore()

    def peer_of(k):
        return lax.rem(y + k // NZ, NY) * NZ + lax.rem(z + k % NZ, NZ)

    def eight(place):
        return pl.ds(pl.multiple_of(place * 8, 8), 8)

    def mem_peer(k):
        return {"mem": lax.rem(mem + k, NM)}

    def send(source, target, send_sem, recv_sem, device):
        copy = pltpu.make_async_remote_copy(
            src_ref=source,
            dst_ref=target,
            send_sem=send_sem,
            recv_sem=recv_sem,
            device_id=device,
            device_id_type=MESH,
        )
        copy.start()
        return copy

    for k in range(1, NM):
        pl.semaphore_signal(barrier, inc=1, device_id=mem_peer(k), device_id_type=MESH)
    for k in range(1, NG):
        pl.semaphore_signal(barrier, inc=1, device_id={"grid": peer_of(k)}, device_id_type=MESH)
    loads = [
        pltpu.make_async_copy(high_hbm, trig_high, local_sem.at[0]),
        pltpu.make_async_copy(low_hbm, trig_low, local_sem.at[1]),
        pltpu.make_async_copy(lead_hbm.at[me], lead, local_sem.at[2]),
    ]
    for copy in loads:
        copy.start()

    for ens, ref in ((0, prior_ref), (1, post_ref)):
        for j in range(HALF):
            for h in range(2):
                sums[ens * 20 + j * 2 + h] = ref[j, h, 0] + ref[j, h, 1]
    left[...] = jnp.zeros_like(left)

    def fill(make):
        for ens in range(2):
            for j in range(HALF):
                north, south = make(ens, j)
                for q, part in ((0, north + south), (1, north - south)):
                    for v in range(LEV):
                        row = (ens * 4 + v * 2 + q) * 16 + j
                        left[row : row + 1, :] = part[v : v + 1, :]
        high, low = split_rows(left[...])
        split[0:128, :] = high
        split[128:256, :] = low

    def fourier(half):
        columns = pl.ds(pl.multiple_of(half * 640, 128), 640)
        both = jnp.dot(split[...], trig_high[:, columns], preferred_element_type=f32)
        return (
            both[0:128]
            + both[128:256]
            + jnp.dot(split[0:128, :], trig_low[:, columns], preferred_element_type=f32)
        )

    def pieces(result, o):
        return [result[x * 16 : x * 16 + 16, o * 40 : o * 40 + 40] for x in range(8)]

    own_half = lax.div(y, 2)
    targets = []
    for step in range(2):
        half = own_half if step == 0 else 1 - own_half
        for j in range(2):
            if step == 0:
                far_y = y if j == 0 else y + 1 - 2 * lax.rem(y, 2)
            else:
                far_y = 2 * half + lax.rem(y + j, 2)
            for dz in (4, 3, 5, 2, 6, 1, 7, 0):
                if step == 0 and j == 0 and dz == 0:
                    continue
                targets.append((step, (step * 2 + j) * 8 + dz, far_y * NZ + lax.rem(z + dz, NZ)))

    def give(part, k, peer, columns):
        return [
            send(
                out_a.at[eight(peer), columns],
                in_a.at[eight(me), columns],
                s_ex.at[part, k],
                r_ex.at[part, k],
                {"grid": peer},
            ),
            send(
                out_b.at[peer, :, columns],
                in_b.at[me, :, columns],
                s_ex.at[part + 1, k],
                r_ex.at[part + 1, k],
                {"grid": peer},
            ),
        ]

    def difference(ens, j):
        ref = (prior_ref, post_ref)[ens]
        return tuple((ref[j, h, 0] - ref[j, h, 1]) * 0.5 for h in range(2))

    fill(difference)
    for copy in loads:
        copy.wait()
    for half in range(2):
        result = fourier(half)
        for o in range(16):
            block = jnp.concatenate(pieces(result, o), axis=1)
            place = half * 16 + o
            out_a[place * 8 : place * 8 + 8, 0:320] = block[0:8]
            out_b[place, :, 0:320] = block[8:10]

    source = lax.broadcasted_iota(jnp.int32, (TROWS, TROWS), 0)
    target = lax.broadcasted_iota(jnp.int32, (TROWS, TROWS), 1)
    small = (target - 256) & 63
    wanted = jnp.where(
        target < 256,
        (target >> 3) * HALF + (target & 7),
        (small >> 1) * HALF + 8 + (small & 1),
    )
    lats_ref[...] = jnp.dot(
        natural_ref[...],
        jnp.where(source == wanted, 1.0, 0.0).astype(f32),
        precision=lax.Precision.HIGHEST,
        preferred_element_type=f32,
    )
    legendre_start, legendre_finish = legendre_parts(me, lead, lats_ref, table, rows, EARLY)

    pl.semaphore_wait(barrier, NM + NG - 2)
    pending = []
    now = []
    for k in range(1, NM):
        peer = lax.rem(mem + k, NM)
        now.append(
            send(
                sums.at[pl.ds(peer * 5, 5)],
                arrived.at[k - 1],
                s_rs.at[k - 1],
                r_rs.at[k - 1],
                mem_peer(k),
            )
        )
    exchanged = []
    for _, k, peer in targets:
        exchanged += give(0, k, peer, pl.ds(0, 256))
    value = sums[pl.ds(mem * 5, 5)]
    for k, copy in enumerate(now):
        copy.wait_recv()
        value = value + arrived[k]
    pending += now
    piece[...] = value * (1.0 / MEMBERS)
    mean_ref[pl.ds(mem * 5, 5)] = piece[...]
    now = [
        send(piece, mean_ref.at[pl.ds(mem * 5, 5)], s_ag.at[k - 1], r_ag.at[k - 1], mem_peer(k))
        for k in range(1, NM)
    ]
    legendre_state = legendre_start()
    for copy in now:
        copy.wait_recv()
    pending += now

    def centred(ens, j):
        return tuple(
            sums[ens * 20 + j * 2 + h] * 0.5 - mean_ref[ens * 20 + j * 2 + h] for h in range(2)
        )

    fill(centred)
    for step in range(2):
        half = own_half if step == 0 else 1 - own_half
        result = fourier(half)
        for o in range(16):
            place = half * 16 + o
            parts = pieces(result, o)
            out_a[eight(place), 256:640] = jnp.concatenate(
                [out_a[eight(place), 256:320]] + [part[0:8] for part in parts], axis=1
            )
            out_b[place, :, 256:640] = jnp.concatenate(
                [out_b[place, :, 256:320]] + [part[8:10] for part in parts], axis=1
            )
        for at, k, peer in targets:
            if at == step:
                exchanged += give(2, k, peer, pl.ds(256, 384))

    legendre_finish(legendre_state)

    in_a[eight(me), :] = out_a[eight(me), :]
    in_b[me] = out_b[me]
    for copy in exchanged:
        copy.wait_recv()
    pending += exchanged
    for g in range(NG):
        two = in_b[g]
        pairs[g * 2 : g * 2 + 2, :] = two
        pairs[64 + g * 2 : 64 + g * 2 + 2, :] = two
    for t in range(2):
        at = t * 128
        turned[t] = in_a[at : at + 128, :].T * lats_ref[1:2, at : at + 128]
    turned[2] = pairs[...].T * lats_ref[1:2, 256:384]
    total[...] = jnp.zeros_like(total)
    lane = lax.broadcasted_iota(jnp.int32, (16, TROWS), 1)

    def analyse_pair(p, odd):
        pair = me * HALF + p
        first_weight = jnp.where(pair == 0, 2.0, 4.0).astype(f32)
        for q in range(2):
            groups = []
            for e in range(2):
                parity = (q + odd + 1 - e) % 2
                for part in range(2):
                    start = parity * 40 + p * 4 + e * 2 + part
                    groups.append(
                        jnp.concatenate(
                            [turned[t, pl.ds(start, 8, stride=80), :] for t in range(3)], axis=1
                        )
                    )
            high, low = split_rows(jnp.concatenate(groups, axis=0))
            operand = jnp.concatenate(
                [
                    jnp.concatenate([high[:, 0:256], high[:, 0:256], high[:, 256:384]], axis=1),
                    jnp.concatenate([low[:, 0:256], low[:, 0:256], low[:, 256:384]], axis=1),
                ],
                axis=0,
            )
            both = lax.dot_general(
                operand,
                table[p * 2 + q],
                (((1,), (1,)), ((), ())),
                preferred_element_type=f32,
            )
            result = both[0:32] + both[32:64]
            in_first = 2 * lane + q < NLAT - pair
            chosen = jnp.where(in_first, result[0:16], result[16:32])
            spectral[p * 2 + q] = chosen
            squares = chosen * chosen
            where = slice(q * TROWS, (q + 1) * TROWS)
            total[0, :, where] += jnp.where(in_first, squares, 0.0) * first_weight
            total[1, :, where] += jnp.where(in_first, 0.0, squares) * 4.0

    def analyse_two(i, carry):
        analyse_pair(2 * i, 0)
        analyse_pair(2 * i + 1, 1)
        return carry

    lax.fori_loop(0, HALF // 2, analyse_two, 0)
    for s in range(2):
        both = total[s, 0:8, :] + total[s, 8:16, :]
        power[s * 4 : s * 4 + 4, 0:768] = both[0:4] + both[4:8]
    power[:, 768:1024] = jnp.zeros((8, 256), f32)

    def lanes(index):
        return pl.ds(pl.multiple_of(index * 128, 128), 128)

    now = [
        send(
            power.at[:, lanes(lax.rem(mem + k, NM))],
            at_m.at[k - 1],
            s_p1.at[k - 1],
            r_p1.at[k - 1],
            mem_peer(k),
        )
        for k in range(1, NM)
    ]
    value = power[:, lanes(mem)]
    for k, copy in enumerate(now):
        copy.wait_recv()
        value = value + at_m[k]
    pending += now

    own[0] = value
    now = [
        send(own.at[0], at_g.at[k - 1], s_p2.at[k - 1], r_p2.at[k - 1], {"grid": peer_of(k)})
        for k in sorted(range(1, NG), key=lambda k: -min(k % NZ, NZ - k % NZ))
    ]
    for copy in now:
        copy.wait_recv()
    value = value + jnp.sum(at_g[...], axis=0)
    pending += now
    own[2] = value
    summed[:, lanes(mem)] = value
    now = [
        send(own.at[2], summed.at[:, lanes(mem)], s_p4.at[k - 1], r_p4.at[k - 1], mem_peer(k))
        for k in range(1, NM)
    ]
    for copy in now:
        copy.wait_recv()
    pending += now

    row = lax.broadcasted_iota(jnp.int32, (TROWS, TROWS), 0)
    column = lax.broadcasted_iota(jnp.int32, (TROWS, TROWS), 1)
    relaxation = jnp.where(
        lax.broadcasted_iota(jnp.int32, (2, TROWS), 0) == 0, relax_ref[0], relax_ref[1]
    )
    place_row = lax.broadcasted_iota(jnp.int32, (2, TROWS), 1)
    odd_row = lax.rem(lax.broadcasted_iota(jnp.int32, (16, TROWS), 0), 2) == 1
    for q in range(2):
        reverse = jnp.where(row + column == 320 - q, 1.0, 0.0).astype(f32)
        part = summed[:, q * TROWS : (q + 1) * TROWS]
        flipped = jnp.dot(
            part, reverse, precision=lax.Precision.HIGHEST, preferred_element_type=f32
        )
        power_prior = flipped[0:2] + part[4:6]
        power_post = flipped[2:4] + part[6:8]
        degree = jnp.maximum(2 * place_row + (q - 1), 0).astype(f32)
        samples = MEMBERS * (2.0 * degree + 1.0)
        spread = (power_prior / samples + EPS) / (power_post / samples + EPS)
        value = (1.0 - relaxation) + relaxation * jnp.sqrt(spread)
        back = jnp.dot(
            jnp.concatenate([value] * 4, axis=0),
            reverse,
            precision=lax.Precision.HIGHEST,
            preferred_element_type=f32,
        )
        ratio[q, 0] = jnp.where(odd_row, back[1:2], back[0:1])
        ratio[q, 1] = jnp.where(odd_row, value[1:2], value[0:1])

    def synth_pair(p, odd):
        pair = me * HALF + p
        for q in range(2):
            in_first = 2 * lane + q < NLAT - pair
            inside = 2 * lane + q <= NLAT
            values = spectral[p * 2 + q]
            high, low = split_rows(
                jnp.concatenate(
                    [
                        jnp.where(in_first, values * ratio[q, 0], 0.0),
                        jnp.where(inside & ~in_first, values * ratio[q, 1], 0.0),
                    ],
                    axis=0,
                )
            )
            both = jnp.dot(
                jnp.concatenate([high, low], axis=0),
                table[p * 2 + q],
                preferred_element_type=f32,
            )
            result = both[0:32] + both[32:64]
            a_part = result[:, 0:256] + result[:, 256:512]
            b_part = result[:, 512:640]
            b_part = b_part + pltpu.roll(b_part, 64, 1)
            for e in range(2):
                parity = (q + odd + 1 - e) % 2
                for part in range(2):
                    for b in range(2):
                        at = e * 16 + part * 8 + b * 4 + 2
                        start = (parity * 4 + b * 2) * 40 + p * 4 + e * 2 + part
                        where = pl.ds(start, 2, stride=40)
                        merged[0, where, :] = a_part[at : at + 2, 0:128]
                        merged[1, where, :] = a_part[at : at + 2, 128:256]
                        merged[2, where, :] = b_part[at : at + 2]

    def synth_two(i, carry):
        synth_pair(2 * i, 0)
        synth_pair(2 * i + 1, 1)
        return carry

    merged[:, 320:384, :] = jnp.zeros((3, 64, 128), f32)
    lax.fori_loop(0, HALF // 2, synth_two, 0)
    for t in range(2):
        ret_a[t * 128 : t * 128 + 128, :] = merged[t].T
    b_rows = merged[2].T
    for g in range(NG):
        ret_b[g] = b_rows[g * 2 : g * 2 + 2, :]

    now = []
    for k in sorted(range(1, NG), key=lambda k: -min(k % NZ, NZ - k % NZ)):
        peer = peer_of(k)
        now.append(
            send(
                ret_a.at[eight(peer), :],
                back_a.at[eight(me), :],
                s_re.at[0, k],
                r_re.at[0, k],
                {"grid": peer},
            )
        )
        now.append(
            send(ret_b.at[peer], back_b.at[me], s_re.at[1, k], r_re.at[1, k], {"grid": peer})
        )
    back_a[eight(me), :] = ret_a[eight(me), :]
    back_b[me] = ret_b[me]
    for copy in now:
        copy.wait()
    for copy in pending:
        copy.wait_send()


def spectral(prior, posterior, natural, relaxation, lead, high, low):
    vmem = pl.BlockSpec(memory_space=pltpu.VMEM)
    hbm = pl.BlockSpec(memory_space=pl.ANY)
    return pl.pallas_call(
        spectral_kernel,
        out_shape=(
            jax.ShapeDtypeStruct((40, LEV, NLON), f32),
            jax.ShapeDtypeStruct((NG * 8, TROWS), f32),
            jax.ShapeDtypeStruct((NG, 2, TROWS), f32),
        ),
        in_specs=[vmem, vmem, vmem, pl.BlockSpec(memory_space=pltpu.SMEM), hbm, hbm, hbm],
        out_specs=(vmem, vmem, vmem),
        scratch_shapes=[
            pltpu.VMEM((40, LEV, NLON), f32),
            pltpu.VMEM((NM - 1, 5, LEV, NLON), f32),
            pltpu.VMEM((5, LEV, NLON), f32),
            pltpu.VMEM((2, 16, 128), f32),
            pltpu.VMEM((NLON, NLON), bf16),
            pltpu.VMEM((NLON, NLON), bf16),
            pltpu.VMEM((128, NLON), f32),
            pltpu.VMEM((256, NLON), bf16),
            pltpu.VMEM((8, TROWS), f32),
            pltpu.VMEM((NG * 8, 640), f32),
            pltpu.VMEM((NG, 2, 640), f32),
            pltpu.VMEM((NG * 8, 640), f32),
            pltpu.VMEM((NG, 2, 640), f32),
            pltpu.VMEM((3, 2 * SIDE, 128), f32),
            pltpu.VMEM((2 * HALF, TROWS, 640), bf16),
            pltpu.VMEM((128, 640), f32),
            pltpu.VMEM((3, 640, 128), f32),
            pltpu.VMEM((2, 16, 2 * TROWS), f32),
            pltpu.VMEM((2 * HALF, 16, TROWS), f32),
            pltpu.VMEM((8, 1024), f32),
            pltpu.VMEM((8, 1024), f32),
            pltpu.VMEM((3, 8, 128), f32),
            pltpu.VMEM((NM - 1, 8, 128), f32),
            pltpu.VMEM((NG - 1, 8, 128), f32),
            pltpu.VMEM((2, 2, 16, TROWS), f32),
            pltpu.VMEM((3, TROWS, 128), f32),
            pltpu.VMEM((NG * 8, TROWS), f32),
            pltpu.VMEM((NG, 2, TROWS), f32),
            pltpu.SemaphoreType.DMA((3,)),
        ]
        + [pltpu.SemaphoreType.DMA((NM - 1,)) for _ in range(4)]
        + [pltpu.SemaphoreType.DMA((4, NG)) for _ in range(2)]
        + [pltpu.SemaphoreType.DMA((n - 1,)) for n in (NM, NM, NG, NG, NM, NM)]
        + [pltpu.SemaphoreType.DMA((2, NG)) for _ in range(2)],
        compiler_params=pltpu.CompilerParams(
            collective_id=0, has_side_effects=True, vmem_limit_bytes=BIG
        ),
        name="spectral",
    )(prior, posterior, natural, relaxation, lead, high, low)


def inverse_kernel(src_a, src_b, mean_ref, high_ref, low_ref, out_ref, split, joined):
    @pl.when(pl.program_id(0) == 0)
    def _():
        for o in range(NG):
            joined[o * 16 : o * 16 + 8, :] = src_a[o * 8 : o * 8 + 8, :]
            joined[o * 16 + 8 : o * 16 + 10, :] = src_b[o]
            joined[o * 16 + 10 : o * 16 + 16, :] = jnp.zeros((6, TROWS), f32)
        for x in range(8):
            row = jnp.concatenate(
                [
                    joined[o * 16 : o * 16 + 16, x * 40 : x * 40 + 40]
                    for o in range(NG)
                ],
                axis=1,
            )
            high, low = split_rows(row)
            split[x * 16 : x * 16 + 16, :] = high
            split[128 + x * 16 : 128 + x * 16 + 16, :] = low

    both = jnp.dot(split[...], high_ref[...], preferred_element_type=f32)
    result = both[0:128] + both[128:256]
    result = result + jnp.dot(split[0:128, :], low_ref[...], preferred_element_type=f32)
    north = result[0:64] + result[64:128]
    south = result[0:64] - result[64:128]
    for h, part in ((0, north), (1, south)):
        members = (part[32:64] + part[0:32], part[32:64] - part[0:32])
        for j in range(HALF):
            mean = mean_ref[20 + j * 2 + h]
            for b in range(2):
                for v in range(LEV):
                    row = v * 16 + j
                    out_ref[j, h, b, v : v + 1, :] = (
                        members[b][row : row + 1, :] + mean[v : v + 1, :]
                    )


def inverse_fourier(returned, mean, high, low):
    width = 640
    return pl.pallas_call(
        inverse_kernel,
        grid=(NLON // width,),
        out_shape=jax.ShapeDtypeStruct((HALF, 2, 2, LEV, NLON), f32),
        in_specs=[
            pl.BlockSpec((NG * 8, TROWS), lambda i: (0, 0)),
            pl.BlockSpec((NG, 2, TROWS), lambda i: (0, 0, 0)),
            pl.BlockSpec((40, LEV, width), lambda i: (0, 0, i)),
            pl.BlockSpec((NLON, width), lambda i: (0, i)),
            pl.BlockSpec((NLON, width), lambda i: (0, i)),
        ],
        out_specs=pl.BlockSpec((HALF, 2, 2, LEV, width), lambda i: (0, 0, 0, 0, i)),
        scratch_shapes=[pltpu.VMEM((256, NLON), bf16), pltpu.VMEM((NG * 16, TROWS), f32)],
        compiler_params=pltpu.CompilerParams(vmem_limit_bytes=BIG),
        name="inverse_fourier",
    )(*returned, mean, high, low)


def per_device(prior, posterior, cycle_rows, relaxation):
    forward_high, forward_low, inverse_high, inverse_low = (jnp.asarray(t) for t in trig_tables())
    colatitude = math.pi * (cycle_rows.reshape(1, NPAIR).astype(f32) + 0.5) / NLAT
    sines = jnp.sin(colatitude)
    lats = jnp.concatenate([jnp.cos(colatitude), math.pi / NLAT * sines, jnp.log(sines)], axis=0)
    lats = jnp.pad(lats, ((0, 5), (0, TROWS - NPAIR)))
    mean, back_a, back_b = spectral(
        prior, posterior, lats, relaxation, jnp.asarray(leading_logs()), forward_high, forward_low
    )
    return inverse_fourier((back_a, back_b), mean, inverse_high, inverse_low)


def solution(mesh):
    return jax.shard_map(
        per_device,
        mesh=mesh,
        in_specs=(P("grid", None, "mem", None, None), P("grid", None, "mem", None, None), P(), P()),
        out_specs=P("grid", None, "mem", None, None),
        check_vma=False,
    )
```

```python
import functools
import math

import jax
import jax.numpy as jnp
import ml_dtypes
import numpy as np
from jax import lax
from jax.experimental import pallas as pl
from jax.experimental.pallas import tpu as pltpu
from jax.sharding import PartitionSpec as P

MESH = pl.DeviceIdType.MESH
NLAT = 640
LEV = 2
NLON = 1280
NPAIR = 320
MEMBERS = 16
NG = 32
NM = 8
NY = 4
NZ = 8
HALF = 10
EPS = 1e-06
ROWS = 672
TROWS = 384
PITCH = 17
EARLY = 32
SIDE = 5720
BIG = 60 * 1024 * 1024

f32 = jnp.float32
bf16 = jnp.bfloat16


def split_table(table):
    hi = table.astype(np.float32).astype(ml_dtypes.bfloat16)
    lo = (table - hi.astype(np.float64)).astype(np.float32).astype(ml_dtypes.bfloat16)
    return hi, lo


@functools.lru_cache(maxsize=None)
def trig_tables():
    owner = np.arange(NG)[:, None, None]
    pair = np.arange(HALF)[None, :, None]
    segment = np.arange(2)[None, None, :]
    first = owner * HALF + pair
    order = np.where(segment == 0, first, NLAT - 1 - first).reshape(-1)
    phase = (np.arange(NLON)[:, None] * order[None, :]) % NLON
    angle = 2.0 * np.pi / NLON * phase
    table = np.stack([np.cos(angle), -np.sin(angle)], axis=-1).reshape(NLON, NLON)
    weight = np.repeat(np.where(order == 0, 1.0, 2.0) / NLON, 2)
    return split_table(table) + split_table((table * weight[None, :]).T)


@functools.lru_cache(maxsize=None)
def leading_logs():
    i = np.arange(1, NLAT + 1, dtype=np.float64)
    total = np.concatenate([[0.0], np.cumsum(np.log((2 * i - 1) / (2 * i)))])[:NLAT]
    m = np.arange(NLAT, dtype=np.float64)
    leading = 0.5 * (np.log((2 * m + 1) / 2) + total)
    pair = np.arange(NG)[:, None] * HALF + np.arange(16)[None, :]
    orders = np.clip(np.stack([pair, NLAT - 1 - pair], axis=1), 0, NLAT - 1)
    return np.ascontiguousarray(
        np.broadcast_to(leading[orders][..., None], (NG, 2, 16, 128)).astype(np.float32)
    )


def split_rows(values):
    high = values.astype(bf16)
    low = (values - high.astype(f32)).astype(bf16)
    return high, low


def place_of(side, index):
    return side * SIDE + index * PITCH


def legendre_parts(place, lead_ref, lats_ref, table_ref, rows, early):
    zero = jnp.zeros((16, TROWS), f32)
    sub = lax.broadcasted_iota(jnp.int32, (16, 128), 0)
    step = lax.rem(lax.broadcasted_iota(jnp.int32, (16, 128), 1), 8)
    cosine = jnp.broadcast_to(lats_ref[0:1, :], (16, TROWS))
    log_sine = jnp.broadcast_to(lats_ref[2:3, :], (16, TROWS))
    valid = sub < HALF
    pair = jnp.where(valid, place * HALF + sub, 4 * NLAT)

    def chain(segment, first_block, last_block, order, state=None):
        def block(b, state):
            current, earlier, scale_log = state
            degree = (b * 8 + step).astype(f32)
            m = order.astype(f32)
            inside = valid & (b * 8 + step > order)
            square = degree * degree
            difference = jnp.where(inside, square - m * m, 1.0)
            low = degree - 1.0
            low_square = low * low
            lead = (4.0 * square - 1.0) / difference
            trail = jnp.maximum(low_square - m * m, 0.0) / jnp.maximum(4.0 * low_square - 1.0, 1.0)
            a = jnp.where(inside, jnp.sqrt(jnp.maximum(lead, 0.0)), 0.0)
            c = jnp.where(inside, a * jnp.sqrt(trail), 0.0)
            scale = jnp.exp(scale_log)
            for k in range(8):
                ak = jnp.broadcast_to(a[:, k : k + 1], (16, TROWS))
                ck = jnp.broadcast_to(c[:, k : k + 1], (16, TROWS))
                following = (ak * cosine) * current - ck * earlier
                begin = order == b * 8 + k
                following = jnp.where(jnp.concatenate([begin] * 3, axis=1), 1.0, following)
                earlier = current
                current = following
                entry = current * scale
                degree_now = b * 8 + k
                side = (k + 1) % 2
                if segment == 0:
                    offset = place_of(side, (NLAT - 1 - k - side) // 2 - 4 * b)
                else:
                    offset = place_of(side, 4 * b + (k + 1 - side) // 2)
                    second = degree_now >= NLAT - 1 - pair
                for t in range(3):
                    tile = entry[:, t * 128 : t * 128 + 128]
                    if segment == 1:
                        tile = jnp.where(second, tile, rows[t, pl.ds(offset, 16), :])
                    rows[t, pl.ds(offset, 16), :] = tile
            large = jnp.abs(current) > 1e10
            current = jnp.where(large, current * 1e-20, current)
            earlier = jnp.where(large, earlier * 1e-20, earlier)
            scale_log = jnp.where(large, scale_log + 20.0 * math.log(10.0), scale_log)
            return current, earlier, scale_log

        leading = jnp.concatenate([lead_ref[segment]] * 3, axis=1)
        wide = jnp.concatenate([order.astype(f32)] * 3, axis=1)
        if state is None:
            state = (zero, zero, leading + wide * log_sine)
        return lax.fori_loop(first_block, last_block, block, state)

    begin_block = lax.div(place * HALF, 8)
    middle = jnp.minimum(begin_block + early, NLAT // 8)

    def start():
        for i in range(641, ROWS):
            for t in range(3):
                rows[t, pl.ds(place_of(i % 2, i // 2), 16), :] = zero[:, 0:128]
        return chain(0, begin_block, middle, pair)

    def finish(state):
        chain(0, middle, NLAT // 8, pair, state)
        chain(1, lax.div(NLAT - HALF - place * HALF, 8), NLAT // 8, NLAT - 1 - pair)

        right = lax.broadcasted_iota(jnp.int32, (16, 128), 1) < 64
        blank = jnp.zeros((TROWS - ROWS // 2, 640), bf16)
        for p in range(HALF):
            for q in range(2):

                def convert(t, carry):
                    out = pl.ds(pl.multiple_of(t * 16, 16), 16)
                    for tile in range(3):
                        values = rows[tile, pl.ds(q * SIDE + t * 16 * PITCH + p, 16, stride=PITCH), :]
                        high = values.astype(bf16)
                        low = values - high.astype(f32)
                        if tile < 2:
                            at = tile * 128
                            table_ref[p * 2 + q, out, at : at + 128] = high
                            table_ref[p * 2 + q, out, at + 256 : at + 384] = low.astype(bf16)
                        else:
                            table_ref[p * 2 + q, out, 512:640] = jnp.where(right, values, low).astype(bf16)
                    return carry

                lax.fori_loop(0, ROWS // 32, convert, 0, unroll=3)
                table_ref[p * 2 + q, ROWS // 2 : TROWS, :] = blank

    return start, finish


def spectral_kernel(
    prior_ref,
    post_ref,
    natural_ref,
    relax_ref,
    lead_hbm,
    high_hbm,
    low_hbm,
    mean_ref,
    back_a,
    back_b,
    sums,
    arrived,
    piece,
    lead,
    trig_high,
    trig_low,
    left,
    split,
    lats_ref,
    out_a,
    out_b,
    in_a,
    in_b,
    rows,
    table,
    pairs,
    turned,
    total,
    spectral,
    power,
    summed,
    own,
    at_m,
    at_g,
    ratio,
    merged,
    ret_a,
    ret_b,
    packed,
    last,
    local_sem,
    s_rs,
    r_rs,
    s_ag,
    r_ag,
    s_ex,
    r_ex,
    s_p1,
    r_p1,
    s_p2,
    r_p2,
    s_p4,
    r_p4,
    s_re,
    r_re,
):
    mem = lax.axis_index("mem")
    me = lax.axis_index("grid")
    y, z = lax.div(me, NZ), lax.rem(me, NZ)
    barrier = pltpu.get_barrier_semaphore()

    def peer_of(k):
        return lax.rem(y + k // NZ, NY) * NZ + lax.rem(z + k % NZ, NZ)

    def eight(place):
        return pl.ds(pl.multiple_of(place * 8, 8), 8)

    def mem_peer(k):
        return {"mem": lax.rem(mem + k, NM)}

    def send(source, target, send_sem, recv_sem, device):
        copy = pltpu.make_async_remote_copy(
            src_ref=source,
            dst_ref=target,
            send_sem=send_sem,
            recv_sem=recv_sem,
            device_id=device,
            device_id_type=MESH,
        )
        copy.start()
        return copy

    for k in range(1, NM):
        pl.semaphore_signal(barrier, inc=1, device_id=mem_peer(k), device_id_type=MESH)
    for k in range(1, NG):
        pl.semaphore_signal(barrier, inc=1, device_id={"grid": peer_of(k)}, device_id_type=MESH)
    loads = [
        pltpu.make_async_copy(high_hbm, trig_high, local_sem.at[0]),
        pltpu.make_async_copy(low_hbm, trig_low, local_sem.at[1]),
        pltpu.make_async_copy(lead_hbm.at[me], lead, local_sem.at[2]),
    ]
    for copy in loads:
        copy.start()

    for ens, ref in ((0, prior_ref), (1, post_ref)):
        for j in range(HALF):
            for h in range(2):
                sums[ens * 20 + j * 2 + h] = ref[j, h, 0] + ref[j, h, 1]
    left[...] = jnp.zeros_like(left)

    def fill(make):
        for ens in range(2):
            for j in range(HALF):
                north, south = make(ens, j)
                for q, part in ((0, north + south), (1, north - south)):
                    for v in range(LEV):
                        row = (ens * 4 + v * 2 + q) * 16 + j
                        left[row : row + 1, :] = part[v : v + 1, :]
        high, low = split_rows(left[...])
        split[0:128, :] = high
        split[128:256, :] = low

    def fourier(half):
        columns = pl.ds(pl.multiple_of(half * 640, 128), 640)
        both = jnp.dot(split[...], trig_high[:, columns], preferred_element_type=f32)
        return (
            both[0:128]
            + both[128:256]
            + jnp.dot(split[0:128, :], trig_low[:, columns], preferred_element_type=f32)
        )

    def pieces(result, o):
        return [result[x * 16 : x * 16 + 16, o * 40 : o * 40 + 40] for x in range(8)]

    own_half = lax.div(y, 2)
    targets = []
    for step in range(2):
        half = own_half if step == 0 else 1 - own_half
        for j in range(2):
            if step == 0:
                far_y = y if j == 0 else y + 1 - 2 * lax.rem(y, 2)
            else:
                far_y = 2 * half + lax.rem(y + j, 2)
            for dz in (4, 3, 5, 2, 6, 1, 7, 0):
                if step == 0 and j == 0 and dz == 0:
                    continue
                targets.append((step, (step * 2 + j) * 8 + dz, far_y * NZ + lax.rem(z + dz, NZ)))

    def give(part, k, peer, columns):
        return [
            send(
                out_a.at[eight(peer), columns],
                in_a.at[eight(me), columns],
                s_ex.at[part, k],
                r_ex.at[part, k],
                {"grid": peer},
            ),
            send(
                out_b.at[peer, :, columns],
                in_b.at[me, :, columns],
                s_ex.at[part + 1, k],
                r_ex.at[part + 1, k],
                {"grid": peer},
            ),
        ]

    def difference(ens, j):
        ref = (prior_ref, post_ref)[ens]
        return tuple((ref[j, h, 0] - ref[j, h, 1]) * 0.5 for h in range(2))

    fill(difference)
    for copy in loads:
        copy.wait()
    for half in range(2):
        result = fourier(half)
        for o in range(16):
            block = jnp.concatenate(pieces(result, o), axis=1)
            place = half * 16 + o
            out_a[place * 8 : place * 8 + 8, 0:320] = block[0:8]
            out_b[place, :, 0:320] = block[8:10]

    source = lax.broadcasted_iota(jnp.int32, (TROWS, TROWS), 0)
    target = lax.broadcasted_iota(jnp.int32, (TROWS, TROWS), 1)
    small = (target - 256) & 63
    wanted = jnp.where(
        target < 256,
        (target >> 3) * HALF + (target & 7),
        (small >> 1) * HALF + 8 + (small & 1),
    )
    lats_ref[...] = jnp.dot(
        natural_ref[...],
        jnp.where(source == wanted, 1.0, 0.0).astype(f32),
        precision=lax.Precision.HIGHEST,
        preferred_element_type=f32,
    )
    legendre_start, legendre_finish = legendre_parts(me, lead, lats_ref, table, rows, EARLY)

    pl.semaphore_wait(barrier, NM + NG - 2)
    pending = []
    now = []
    for k in range(1, NM):
        peer = lax.rem(mem + k, NM)
        now.append(
            send(
                sums.at[pl.ds(peer * 5, 5)],
                arrived.at[k - 1],
                s_rs.at[k - 1],
                r_rs.at[k - 1],
                mem_peer(k),
            )
        )
    exchanged = []
    for _, k, peer in targets:
        exchanged += give(0, k, peer, pl.ds(0, 256))
    value = sums[pl.ds(mem * 5, 5)]
    for k, copy in enumerate(now):
        copy.wait_recv()
        value = value + arrived[k]
    pending += now
    piece[...] = value * (1.0 / MEMBERS)
    mean_ref[pl.ds(mem * 5, 5)] = piece[...]
    now = [
        send(piece, mean_ref.at[pl.ds(mem * 5, 5)], s_ag.at[k - 1], r_ag.at[k - 1], mem_peer(k))
        for k in range(1, NM)
    ]
    legendre_state = legendre_start()
    for copy in now:
        copy.wait_recv()
    pending += now

    def centred(ens, j):
        return tuple(
            sums[ens * 20 + j * 2 + h] * 0.5 - mean_ref[ens * 20 + j * 2 + h] for h in range(2)
        )

    fill(centred)
    for step in range(2):
        half = own_half if step == 0 else 1 - own_half
        result = fourier(half)
        for o in range(16):
            place = half * 16 + o
            parts = pieces(result, o)
            out_a[eight(place), 256:640] = jnp.concatenate(
                [out_a[eight(place), 256:320]] + [part[0:8] for part in parts], axis=1
            )
            out_b[place, :, 256:640] = jnp.concatenate(
                [out_b[place, :, 256:320]] + [part[8:10] for part in parts], axis=1
            )
        for at, k, peer in targets:
            if at == step:
                exchanged += give(2, k, peer, pl.ds(256, 384))

    legendre_finish(legendre_state)

    in_a[eight(me), :] = out_a[eight(me), :]
    in_b[me] = out_b[me]
    for copy in exchanged:
        copy.wait_recv()
    pending += exchanged
    for g in range(NG):
        two = in_b[g]
        pairs[g * 2 : g * 2 + 2, :] = two
        pairs[64 + g * 2 : 64 + g * 2 + 2, :] = two
    for t in range(2):
        at = t * 128
        turned[t] = in_a[at : at + 128, :].T * lats_ref[1:2, at : at + 128]
    turned[2] = pairs[...].T * lats_ref[1:2, 256:384]
    total[...] = jnp.zeros_like(total)
    lane = lax.broadcasted_iota(jnp.int32, (16, TROWS), 1)

    def analyse_pair(p, odd):
        pair = me * HALF + p
        first_weight = jnp.where(pair == 0, 2.0, 4.0).astype(f32)
        for q in range(2):
            groups = []
            for e in range(2):
                parity = (q + odd + 1 - e) % 2
                for part in range(2):
                    start = parity * 40 + p * 4 + e * 2 + part
                    groups.append(
                        jnp.concatenate(
                            [turned[t, pl.ds(start, 8, stride=80), :] for t in range(3)], axis=1
                        )
                    )
            high, low = split_rows(jnp.concatenate(groups, axis=0))
            operand = jnp.concatenate(
                [
                    jnp.concatenate([high[:, 0:256], high[:, 0:256], high[:, 256:384]], axis=1),
                    jnp.concatenate([low[:, 0:256], low[:, 0:256], low[:, 256:384]], axis=1),
                ],
                axis=0,
            )
            both = lax.dot_general(
                operand,
                table[p * 2 + q],
                (((1,), (1,)), ((), ())),
                preferred_element_type=f32,
            )
            result = both[0:32] + both[32:64]
            in_first = 2 * lane + q < NLAT - pair
            chosen = jnp.where(in_first, result[0:16], result[16:32])
            spectral[p * 2 + q] = chosen
            squares = chosen * chosen
            where = slice(q * TROWS, (q + 1) * TROWS)
            total[0, :, where] += jnp.where(in_first, squares, 0.0) * first_weight
            total[1, :, where] += jnp.where(in_first, 0.0, squares) * 4.0

    def analyse_two(i, carry):
        analyse_pair(2 * i, 0)
        analyse_pair(2 * i + 1, 1)
        return carry

    lax.fori_loop(0, HALF // 2, analyse_two, 0)
    for s in range(2):
        both = total[s, 0:8, :] + total[s, 8:16, :]
        power[s * 4 : s * 4 + 4, 0:768] = both[0:4] + both[4:8]
    power[:, 768:1024] = jnp.zeros((8, 256), f32)

    def lanes(index):
        return pl.ds(pl.multiple_of(index * 128, 128), 128)

    now = [
        send(
            power.at[:, lanes(lax.rem(mem + k, NM))],
            at_m.at[k - 1],
            s_p1.at[k - 1],
            r_p1.at[k - 1],
            mem_peer(k),
        )
        for k in range(1, NM)
    ]
    value = power[:, lanes(mem)]
    for k, copy in enumerate(now):
        copy.wait_recv()
        value = value + at_m[k]
    pending += now

    own[0] = value
    now = [
        send(own.at[0], at_g.at[k - 1], s_p2.at[k - 1], r_p2.at[k - 1], {"grid": peer_of(k)})
        for k in sorted(range(1, NG), key=lambda k: -min(k % NZ, NZ - k % NZ))
    ]
    for copy in now:
        copy.wait_recv()
    value = value + jnp.sum(at_g[...], axis=0)
    pending += now
    own[2] = value
    summed[:, lanes(mem)] = value
    now = [
        send(own.at[2], summed.at[:, lanes(mem)], s_p4.at[k - 1], r_p4.at[k - 1], mem_peer(k))
        for k in range(1, NM)
    ]
    for copy in now:
        copy.wait_recv()
    pending += now

    row = lax.broadcasted_iota(jnp.int32, (TROWS, TROWS), 0)
    column = lax.broadcasted_iota(jnp.int32, (TROWS, TROWS), 1)
    relaxation = jnp.where(
        lax.broadcasted_iota(jnp.int32, (2, TROWS), 0) == 0, relax_ref[0], relax_ref[1]
    )
    place_row = lax.broadcasted_iota(jnp.int32, (2, TROWS), 1)
    odd_row = lax.rem(lax.broadcasted_iota(jnp.int32, (16, TROWS), 0), 2) == 1
    for q in range(2):
        reverse = jnp.where(row + column == 320 - q, 1.0, 0.0).astype(f32)
        part = summed[:, q * TROWS : (q + 1) * TROWS]
        flipped = jnp.dot(
            part, reverse, precision=lax.Precision.HIGHEST, preferred_element_type=f32
        )
        power_prior = flipped[0:2] + part[4:6]
        power_post = flipped[2:4] + part[6:8]
        degree = jnp.maximum(2 * place_row + (q - 1), 0).astype(f32)
        samples = MEMBERS * (2.0 * degree + 1.0)
        spread = (power_prior / samples + EPS) / (power_post / samples + EPS)
        value = (1.0 - relaxation) + relaxation * jnp.sqrt(spread)
        back = jnp.dot(
            jnp.concatenate([value] * 4, axis=0),
            reverse,
            precision=lax.Precision.HIGHEST,
            preferred_element_type=f32,
        )
        ratio[q, 0] = jnp.where(odd_row, back[1:2], back[0:1])
        ratio[q, 1] = jnp.where(odd_row, value[1:2], value[0:1])

    def synth_pair(p, odd):
        pair = me * HALF + p
        for q in range(2):
            in_first = 2 * lane + q < NLAT - pair
            inside = 2 * lane + q <= NLAT
            values = spectral[p * 2 + q]
            high, low = split_rows(
                jnp.concatenate(
                    [
                        jnp.where(in_first, values * ratio[q, 0], 0.0),
                        jnp.where(inside & ~in_first, values * ratio[q, 1], 0.0),
                    ],
                    axis=0,
                )
            )
            both = jnp.dot(
                jnp.concatenate([high, low], axis=0),
                table[p * 2 + q],
                preferred_element_type=f32,
            )
            result = both[0:32] + both[32:64]
            a_part = result[:, 0:256] + result[:, 256:512]
            b_part = result[:, 512:640]
            b_part = b_part + pltpu.roll(b_part, 64, 1)
            for e in range(2):
                parity = (q + odd + 1 - e) % 2
                for part in range(2):
                    for b in range(2):
                        at = e * 16 + part * 8 + b * 4 + 2
                        start = (parity * 4 + b * 2) * 40 + p * 4 + e * 2 + part
                        where = pl.ds(start, 2, stride=40)
                        merged[0, where, :] = a_part[at : at + 2, 0:128]
                        merged[1, where, :] = a_part[at : at + 2, 128:256]
                        merged[2, where, :] = b_part[at : at + 2]

    def synth_two(i, carry):
        synth_pair(2 * i, 0)
        synth_pair(2 * i + 1, 1)
        return carry

    merged[:, 320:384, :] = jnp.zeros((3, 64, 128), f32)
    lax.fori_loop(0, HALF // 2, synth_two, 0)
    b_rows = merged[2].T[0:64]
    for c in range(4):
        tile = b_rows[:, (c // 2) * 128 : (c // 2) * 128 + 128]
        packed[pl.ds(c, 64, stride=4), :] = tile if c % 2 else pltpu.roll(tile, 64, 1)
    last[...] = b_rows[:, 256:384]
    left_half = lax.broadcasted_iota(jnp.int32, (128, 128), 1) < 64
    ends = jnp.where(
        left_half[0:NG],
        last[pl.ds(0, NG, stride=2), :],
        pltpu.roll(last[pl.ds(1, NG, stride=2), :], 64, 1),
    )
    for g in range(NG):
        ret_b[g] = ends[g : g + 1, :]
    for t in range(2):
        at = t * 128
        a_rows = merged[t].T
        ret_a[at : at + 128, 0:256] = a_rows[:, 0:256]
        ret_a[at : at + 128, 256:384] = jnp.where(
            left_half, a_rows[:, 256:384], packed[at : at + 128, :]
        )

    now = []
    for k in sorted(range(1, NG), key=lambda k: -min(k % NZ, NZ - k % NZ)):
        peer = peer_of(k)
        now.append(
            send(
                ret_a.at[eight(peer), :],
                back_a.at[eight(me), :],
                s_re.at[0, k],
                r_re.at[0, k],
                {"grid": peer},
            )
        )
        now.append(
            send(ret_b.at[peer], back_b.at[me], s_re.at[1, k], r_re.at[1, k], {"grid": peer})
        )
    back_a[eight(me), :] = ret_a[eight(me), :]
    back_b[me] = ret_b[me]
    for copy in now:
        copy.wait()
    for copy in pending:
        copy.wait_send()


def spectral(prior, posterior, natural, relaxation, lead, high, low):
    vmem = pl.BlockSpec(memory_space=pltpu.VMEM)
    hbm = pl.BlockSpec(memory_space=pl.ANY)
    return pl.pallas_call(
        spectral_kernel,
        out_shape=(
            jax.ShapeDtypeStruct((40, LEV, NLON), f32),
            jax.ShapeDtypeStruct((NG * 8, TROWS), f32),
            jax.ShapeDtypeStruct((NG, 1, 128), f32),
        ),
        in_specs=[vmem, vmem, vmem, pl.BlockSpec(memory_space=pltpu.SMEM), hbm, hbm, hbm],
        out_specs=(vmem, vmem, vmem),
        scratch_shapes=[
            pltpu.VMEM((40, LEV, NLON), f32),
            pltpu.VMEM((NM - 1, 5, LEV, NLON), f32),
            pltpu.VMEM((5, LEV, NLON), f32),
            pltpu.VMEM((2, 16, 128), f32),
            pltpu.VMEM((NLON, NLON), bf16),
            pltpu.VMEM((NLON, NLON), bf16),
            pltpu.VMEM((128, NLON), f32),
            pltpu.VMEM((256, NLON), bf16),
            pltpu.VMEM((8, TROWS), f32),
            pltpu.VMEM((NG * 8, 640), f32),
            pltpu.VMEM((NG, 2, 640), f32),
            pltpu.VMEM((NG * 8, 640), f32),
            pltpu.VMEM((NG, 2, 640), f32),
            pltpu.VMEM((3, 2 * SIDE, 128), f32),
            pltpu.VMEM((2 * HALF, TROWS, 640), bf16),
            pltpu.VMEM((128, 640), f32),
            pltpu.VMEM((3, 640, 128), f32),
            pltpu.VMEM((2, 16, 2 * TROWS), f32),
            pltpu.VMEM((2 * HALF, 16, TROWS), f32),
            pltpu.VMEM((8, 1024), f32),
            pltpu.VMEM((8, 1024), f32),
            pltpu.VMEM((3, 8, 128), f32),
            pltpu.VMEM((NM - 1, 8, 128), f32),
            pltpu.VMEM((NG - 1, 8, 128), f32),
            pltpu.VMEM((2, 2, 16, TROWS), f32),
            pltpu.VMEM((3, TROWS, 128), f32),
            pltpu.VMEM((NG * 8, TROWS), f32),
            pltpu.VMEM((NG, 1, 128), f32),
            pltpu.VMEM((256, 128), f32),
            pltpu.VMEM((64, 128), f32),
            pltpu.SemaphoreType.DMA((3,)),
        ]
        + [pltpu.SemaphoreType.DMA((NM - 1,)) for _ in range(4)]
        + [pltpu.SemaphoreType.DMA((4, NG)) for _ in range(2)]
        + [pltpu.SemaphoreType.DMA((n - 1,)) for n in (NM, NM, NG, NG, NM, NM)]
        + [pltpu.SemaphoreType.DMA((2, NG)) for _ in range(2)],
        compiler_params=pltpu.CompilerParams(
            collective_id=0, has_side_effects=True, vmem_limit_bytes=BIG
        ),
        name="spectral",
    )(prior, posterior, natural, relaxation, lead, high, low)


def inverse_kernel(
    src_a, src_b, mean_ref, high_ref, low_ref, out_ref, split, joined, spread, both_rows
):
    @pl.when(pl.program_id(0) == 0)
    def _():
        spread[...] = src_a[:, 256:384]
        left_half = lax.broadcasted_iota(jnp.int32, (64, 128), 1) < 64
        found = [spread[pl.ds(c, 64, stride=4), :] for c in range(4)]
        for o in range(NG):
            end = src_b[o]
            both_rows[o * 2 : o * 2 + 1, :] = end
            both_rows[o * 2 + 1 : o * 2 + 2, :] = pltpu.roll(end, 64, 1)
        b_rows = jnp.concatenate(
            [
                jnp.where(left_half, pltpu.roll(found[0], 64, 1), found[1]),
                jnp.where(left_half, pltpu.roll(found[2], 64, 1), found[3]),
                both_rows[...],
            ],
            axis=1,
        )
        for o in range(NG):
            joined[o * 16 : o * 16 + 8, :] = src_a[o * 8 : o * 8 + 8, :]
            joined[o * 16 + 8 : o * 16 + 10, :] = b_rows[o * 2 : o * 2 + 2, :]
            joined[o * 16 + 10 : o * 16 + 16, :] = jnp.zeros((6, TROWS), f32)
        for x in range(8):
            row = jnp.concatenate(
                [
                    joined[o * 16 : o * 16 + 16, x * 40 : x * 40 + 40]
                    for o in range(NG)
                ],
                axis=1,
            )
            high, low = split_rows(row)
            split[x * 16 : x * 16 + 16, :] = high
            split[128 + x * 16 : 128 + x * 16 + 16, :] = low

    both = jnp.dot(split[...], high_ref[...], preferred_element_type=f32)
    result = both[0:128] + both[128:256]
    result = result + jnp.dot(split[0:128, :], low_ref[...], preferred_element_type=f32)
    north = result[0:64] + result[64:128]
    south = result[0:64] - result[64:128]
    for h, part in ((0, north), (1, south)):
        members = (part[32:64] + part[0:32], part[32:64] - part[0:32])
        for j in range(HALF):
            mean = mean_ref[20 + j * 2 + h]
            for b in range(2):
                for v in range(LEV):
                    row = v * 16 + j
                    out_ref[j, h, b, v : v + 1, :] = (
                        members[b][row : row + 1, :] + mean[v : v + 1, :]
                    )


def inverse_fourier(returned, mean, high, low):
    width = 640
    return pl.pallas_call(
        inverse_kernel,
        grid=(NLON // width,),
        out_shape=jax.ShapeDtypeStruct((HALF, 2, 2, LEV, NLON), f32),
        in_specs=[
            pl.BlockSpec((NG * 8, TROWS), lambda i: (0, 0)),
            pl.BlockSpec((NG, 1, 128), lambda i: (0, 0, 0)),
            pl.BlockSpec((40, LEV, width), lambda i: (0, 0, i)),
            pl.BlockSpec((NLON, width), lambda i: (0, i)),
            pl.BlockSpec((NLON, width), lambda i: (0, i)),
        ],
        out_specs=pl.BlockSpec((HALF, 2, 2, LEV, width), lambda i: (0, 0, 0, 0, i)),
        scratch_shapes=[
            pltpu.VMEM((256, NLON), bf16),
            pltpu.VMEM((NG * 16, TROWS), f32),
            pltpu.VMEM((256, 128), f32),
            pltpu.VMEM((64, 128), f32),
        ],
        compiler_params=pltpu.CompilerParams(vmem_limit_bytes=BIG),
        name="inverse_fourier",
    )(*returned, mean, high, low)


def per_device(prior, posterior, cycle_rows, relaxation):
    forward_high, forward_low, inverse_high, inverse_low = (jnp.asarray(t) for t in trig_tables())
    colatitude = math.pi * (cycle_rows.reshape(1, NPAIR).astype(f32) + 0.5) / NLAT
    sines = jnp.sin(colatitude)
    lats = jnp.concatenate([jnp.cos(colatitude), math.pi / NLAT * sines, jnp.log(sines)], axis=0)
    lats = jnp.pad(lats, ((0, 5), (0, TROWS - NPAIR)))
    mean, back_a, back_b = spectral(
        prior, posterior, lats, relaxation, jnp.asarray(leading_logs()), forward_high, forward_low
    )
    return inverse_fourier((back_a, back_b), mean, inverse_high, inverse_low)


def solution(mesh):
    return jax.shard_map(
        per_device,
        mesh=mesh,
        in_specs=(P("grid", None, "mem", None, None), P("grid", None, "mem", None, None), P(), P()),
        out_specs=P("grid", None, "mem", None, None),
        check_vma=False,
    )
```
